32 devices in a mesh: outer: 4 (over y, x), hst: 2 (over core), tp: 4 (over z).
Axes of the slice: x: 2, y: 2, z: 4, core: 2. Of those that a mesh axis runs over, the one named last changes fastest.
Arguments:
- gradient: bfloat16 [8, 2, 8192, 1024], P(('outer', 'hst'), None, None, 'tp'), may hold values from -384 to 384
- error_acc: bfloat16 [8, 2, 8192, 1024], P(('outer', 'hst'), None, None, 'tp'), may hold values from -192 to 192
- q_start: float32 [2, 1024, 32], P(None, 'tp'), may hold values from -6 to 6
Outputs:
- update: bfloat16 [2, 8192, 1024], P(None, None, 'tp')
The draws below stay inside these ranges and needn't reach their ends.
All inputs are finite; a program needn't handle non-finite values.
Results may differ from the reference program's by a relative error of at most 0.008.
Values may be sent and summed in bfloat16 or wider, within the bound.
No kernel may reach another device: no remote copies, remote signals or barrier semaphores. Data moves between devices by JAX's collectives and lax.ppermute only.
A program may use at most 128 MiB of HBM per device.

```python
import jax
import jax.numpy as jnp
from jax import lax

D = 8192
KVW = 1024
RANK = 32
REPLICAS = 8


def block_levels(stream_key, shape, shards, least, top_value):
    level, own = 1.0, jax.random.fold_in(stream_key, 6)
    for dim, shards_of in shards:
        heights = jnp.exp(jax.random.uniform(jax.random.fold_in(own, dim), (shards_of,), jnp.float32, least / len(shards), top_value / len(shards)))
        level = level * jnp.repeat(heights, shape[dim] // shards_of).reshape([-1 if axis == dim else 1 for axis in range(len(shape))])
    return level


def normal_values(own_key, extent, width, reach, cuts=(), kind=jnp.bfloat16):
    loudness = block_levels(own_key, extent, cuts, -0.22, 0.18) if cuts else 1.0
    array = jax.random.normal(own_key, extent, jnp.float32) * width * loudness
    return jnp.minimum(jnp.maximum(array, -reach), reach).astype(kind)


def setup_inputs(seed: int = 0) -> dict:
    key_of = jax.random.split(jax.random.key(seed), 4)
    return {
        "gradient": normal_values(key_of[0], (REPLICAS, 2, D, KVW), 64.0, 384.0, ((0, 8), (3, 4))),
        "error_acc": normal_values(key_of[1], (REPLICAS, 2, D, KVW), 32.0, 192.0, ((0, 8), (3, 4))),
        "q_start": normal_values(key_of[2], (2, KVW, RANK), 1.0, 6.0, ((1, 4),), jnp.float32),
    }


def orthonormal(left):
    gram = jnp.einsum('mdr,mds->mrs', left, left, precision=lax.Precision.HIGHEST)
    lower = jnp.linalg.cholesky(gram)
    return lax.linalg.triangular_solve(lower, left, left_side=False, lower=True, transpose_a=True)

def reference(gradient, error_acc, q_start):
    q_round = q_start.astype(jnp.bfloat16).astype(jnp.float32)

    def mixed_of(index):
        both = gradient[index].astype(jnp.float32) + error_acc[index].astype(jnp.float32)
        return both.astype(jnp.bfloat16).astype(jnp.float32)

    def add_left(carry, index):
        mixed = mixed_of(index)
        return (carry + jnp.einsum('mdk,mkr->mdr', mixed, q_round), None)
    left, unused = lax.scan(add_left, jnp.zeros((2, D, RANK), jnp.float32), jnp.arange(REPLICAS, dtype=jnp.int32))
    basis = orthonormal(left).astype(jnp.bfloat16)
    basis_wide = basis.astype(jnp.float32)

    def add_right(carry, index):
        mixed = mixed_of(index)
        return (carry + jnp.einsum('mdk,mdr->mkr', mixed, basis_wide), None)
    right, unused = lax.scan(add_right, jnp.zeros((2, KVW, RANK), jnp.float32), jnp.arange(REPLICAS, dtype=jnp.int32))
    q_mean = (right / REPLICAS).astype(jnp.bfloat16).astype(jnp.float32)
    return jnp.einsum('mdr,mkr->mdk', basis_wide, q_mean).astype(jnp.bfloat16)
```

```python
import jax
import jax.numpy as jnp
from jax import lax
from jax.experimental import pallas as pl
from jax.experimental.pallas import tpu as pltpu
from jax.sharding import PartitionSpec as P

AXES = ("outer", "hst", "tp")
PACK = 4
LANES = 128
F32, BF16 = jnp.float32, jnp.bfloat16
VMEM_LIMIT = 48 * 1024 * 1024


def bits(size):
    return size.bit_length() - 1


def sizes():
    return tuple(lax.axis_size(axis) for axis in AXES)


def coordinates(index):
    _, hst, tp = sizes()
    return index // (hst * tp), index // tp % hst, index % tp


def exchange(x, partner):
    _, hst, tp = sizes()
    pairs = []
    for index in range(sizes()[0] * hst * tp):
        o, h, t = partner(*coordinates(index))
        pairs.append((index, (o * hst + h) * tp + t))
    return lax.ppermute(x, AXES, pairs)


def replica_steps():
    outer, hst, _ = sizes()
    o, h = lax.axis_index("outer"), lax.axis_index("hst")
    steps = []
    for b in range(bits(hst)):
        steps.append((lambda oo, hh, tt, b=b: (oo, hh ^ (1 << b), tt), (h >> b) & 1))
    n = bits(outer)
    for b in range(n):
        def partner(oo, hh, tt, b=b):
            return oo ^ (1 << (b if hh % 2 == 0 else n - 1 - b)), hh, tt
        steps.append((partner, jnp.where(h % 2 == 0, (o >> b) & 1, (o >> (n - 1 - b)) & 1)))
    return steps


def mix_kernel(q_ref, g_hbm, e_hbm, mixed_ref, left_ref):
    m_count, pack, rows, width = mixed_ref.shape
    block = 256

    def body(g_ref, e_ref):
        i = pl.program_id(0)
        where = pl.ds(pl.multiple_of(i * block, block), block)
        total = jnp.zeros((block, m_count * LANES), F32)
        for m in range(m_count):
            for j in range(pack):
                mixed = (g_ref[m, j].astype(F32) + e_ref[m, j].astype(F32)).astype(BF16)
                mixed_ref[m, j, where, :] = mixed
                total += jnp.dot(mixed, q_ref[m, j], preferred_element_type=F32)
        left_ref[where, :] = total

    spec = pl.BlockSpec((m_count, pack, block, width), lambda i: (0, 0, i, 0))
    pltpu.emit_pipeline(body, grid=(rows // block,), in_specs=[spec, spec])(g_hbm, e_hbm)


def mix(gradient, error_acc, q_start):
    m_count, depth, width = gradient.shape
    rank = q_start.shape[-1]
    rows = depth // PACK
    q_round = q_start.astype(BF16)
    m_eye, j_eye = jnp.eye(m_count, dtype=BF16), jnp.eye(PACK, dtype=BF16)
    wide = q_round[:, None, :, None, None, :] * (m_eye[:, None, None, :, None, None] * j_eye[None, :, None, None, :, None])
    wide = wide.reshape(m_count, PACK, width, m_count * PACK * rank)
    shape = (m_count, PACK, rows, width)
    return pl.pallas_call(
        mix_kernel,
        in_specs=[pl.BlockSpec(memory_space=pltpu.VMEM), pl.BlockSpec(memory_space=pl.ANY), pl.BlockSpec(memory_space=pl.ANY)],
        out_specs=[pl.BlockSpec(memory_space=pltpu.VMEM)] * 2,
        out_shape=[pltpu.VMEM(shape, BF16), pltpu.VMEM((rows, m_count * LANES), F32)],
        compiler_params=pltpu.CompilerParams(vmem_limit_bytes=VMEM_LIMIT),
        name="mix",
    )(wide, gradient.reshape(shape), error_acc.reshape(shape))


def project_kernel(left_ref, mixed_ref, right_ref, gram_ref):
    m_count, pack, rows, width = mixed_ref.shape
    rank = LANES // pack
    left = left_ref[...]
    turned = left.T
    every = jnp.dot(turned, left, preferred_element_type=F32)
    for m in range(m_count):
        gram = jnp.zeros((rank, rank), F32)
        right = jnp.zeros((rank, width), F32)
        for j in range(pack):
            at = m * LANES + j * rank
            gram += every[at:at + rank, at:at + rank]
            right += jnp.dot(turned[at:at + rank], mixed_ref[m, j], preferred_element_type=F32)
        gram_ref[m] = gram
        right_ref[m] = right


def project(left, mixed):
    m_count, pack, rows, width = mixed.shape
    rank = LANES // pack
    return pl.pallas_call(
        project_kernel,
        in_specs=[pl.BlockSpec(memory_space=pltpu.VMEM)] * 2,
        out_specs=[pl.BlockSpec(memory_space=pltpu.VMEM)] * 2,
        out_shape=[pltpu.VMEM((m_count, rank, width), F32), pltpu.VMEM((m_count, rank, rank), F32)],
        compiler_params=pltpu.CompilerParams(vmem_limit_bytes=VMEM_LIMIT),
        name="project",
    )(left, mixed)


def invert_kernel(gram_ref, inverse_ref):
    m_count, rank, _ = gram_ref.shape
    row_at = lax.broadcasted_iota(jnp.int32, (rank, rank), 0)
    col_at = lax.broadcasted_iota(jnp.int32, (rank, rank), 1)
    held = [gram_ref[m] for m in range(m_count)]
    for k in range(rank):
        for m in range(m_count):
            a = held[m]
            row, col = a[k:k + 1, :], a[:, k:k + 1]
            inv = 1.0 / a[k:k + 1, k:k + 1]
            scaled = row * inv
            rest = a - col * scaled
            rest = jnp.where(row_at == k, scaled, rest)
            rest = jnp.where(col_at == k, jnp.where(row_at == k, inv, -col * inv), rest)
            held[m] = rest
    for m in range(m_count):
        inverse_ref[m] = held[m]


def invert(gram):
    return pl.pallas_call(
        invert_kernel,
        in_specs=[pl.BlockSpec(memory_space=pltpu.VMEM)],
        out_specs=pl.BlockSpec(memory_space=pltpu.VMEM),
        out_shape=pltpu.VMEM(gram.shape, F32),
        name="invert",
    )(gram)


def expand_kernel(scale, left_ref, inverse_ref, right_ref, update_ref, wide_ref):
    m_count, rank, width = right_ref.shape
    pack = LANES // rank
    m, half = pl.program_id(0), pl.program_id(1)

    @pl.when((m == 0) & (half == 0))
    def _():
        wide_ref[...] = jnp.zeros_like(wide_ref)
        for mm in range(m_count):
            z = jnp.dot(inverse_ref[mm], right_ref[mm], precision=lax.Precision.HIGHEST, preferred_element_type=F32) * scale
            high = z.astype(BF16)
            low = (z - high.astype(F32)).astype(BF16)
            for j in range(pack):
                wide_ref[mm, j, pl.ds(j * rank, rank), :] = high
                wide_ref[mm, j, pl.ds(LANES + j * rank, rank), :] = low

    left = left_ref[...]
    twice = jnp.concatenate([left, left], axis=1)
    for j in range(pack):
        update_ref[0, j] = jnp.dot(twice, wide_ref[m, j], preferred_element_type=F32).astype(BF16)


def expand(left, inverse, right, scale):
    m_count, rank, width = right.shape
    pack = LANES // rank
    rows = left.shape[0]
    block = rows // 4
    out = pl.pallas_call(
        lambda *refs: expand_kernel(scale, *refs),
        grid=(m_count, rows // block),
        in_specs=[
            pl.BlockSpec((block, LANES), lambda m, i: (i, m)),
            pl.BlockSpec(memory_space=pltpu.VMEM),
            pl.BlockSpec(memory_space=pltpu.VMEM),
        ],
        out_specs=pl.BlockSpec((1, pack, block, width), lambda m, i: (m, 0, i, 0)),
        out_shape=jax.ShapeDtypeStruct((m_count, pack, rows, width), BF16),
        scratch_shapes=[pltpu.VMEM((m_count, pack, 2 * LANES, width), BF16)],
        compiler_params=pltpu.CompilerParams(vmem_limit_bytes=VMEM_LIMIT),
        name="expand",
    )(left, inverse, right)
    return out.reshape(m_count, pack * rows, width)


def sum_left(left):
    steps = replica_steps()
    for partner, bit in steps:
        half = left.shape[0] // 2
        low, high = left[:half], left[half:]
        sent = jnp.where(bit == 1, low, high).astype(BF16)
        kept = jnp.where(bit == 1, high, low)
        left = kept + exchange(sent, partner).astype(F32)
    for b in range(bits(lax.axis_size("tp"))):
        sent = left.astype(BF16)
        left = sent.astype(F32) + exchange(sent, lambda o, h, t, b=b: (o, h, t ^ (1 << b))).astype(F32)
    left = left.astype(BF16)
    for partner, bit in reversed(steps):
        other = exchange(left, partner)
        left = jnp.concatenate([jnp.where(bit == 1, other, left), jnp.where(bit == 1, left, other)])
    return left


def sum_right(right):
    outer, hst, _ = sizes()
    for b in range(bits(hst)):
        right = right + exchange(right, lambda o, h, t, b=b: (o, h ^ (1 << b), t))
    for b in range(bits(outer)):
        right = right + exchange(right, lambda o, h, t, b=b: (o ^ (1 << b), h, t))
    return right


def shards(gradient, error_acc, q_start):
    mixed, left = mix(gradient[0], error_acc[0], q_start)
    left = sum_left(left)
    right, gram = project(left, mixed)
    inverse = invert(gram)
    outer, hst, _ = sizes()
    right = sum_right(right)
    return expand(left, inverse, right, 1.0 / (outer * hst))


def solution(mesh):
    in_specs = (
        P(("outer", "hst"), None, None, "tp"),
        P(("outer", "hst"), None, None, "tp"),
        P(None, "tp", None),
    )
    out_specs = P(None, None, "tp")
    return jax.shard_map(shards, mesh=mesh, in_specs=in_specs, out_specs=out_specs, check_vma=False)
```

```python
import jax
import jax.numpy as jnp
from jax import lax
from jax.experimental import pallas as pl
from jax.experimental.pallas import tpu as pltpu
from jax.sharding import PartitionSpec as P

AXES = ("outer", "hst", "tp")
PACK = 4
LANES = 128
F32, BF16 = jnp.float32, jnp.bfloat16
MIB = 1024 * 1024


def bits(size):
    return size.bit_length() - 1


def sizes():
    return tuple(lax.axis_size(axis) for axis in AXES)


def coordinates(index):
    _, hst, tp = sizes()
    return index // (hst * tp), index // tp % hst, index % tp


def exchange(x, partner):
    _, hst, tp = sizes()
    pairs = []
    for index in range(sizes()[0] * hst * tp):
        o, h, t = partner(*coordinates(index))
        pairs.append((index, (o * hst + h) * tp + t))
    return lax.ppermute(x, AXES, pairs)


def replica_steps():
    outer, hst, _ = sizes()
    steps = []
    for b in range(bits(hst)):
        steps.append((lambda o, h, t, b=b: (o, h ^ (1 << b), t), lambda o, h, b=b: (h >> b) & 1))
    n = bits(outer)
    for b in range(n):
        def partner(o, h, t, b=b):
            return o ^ (1 << (b if h % 2 == 0 else n - 1 - b)), h, t

        def bit(o, h, b=b):
            return jnp.where(h % 2 == 0, (o >> b) & 1, (o >> (n - 1 - b)) & 1)

        steps.append((partner, bit))
    return steps


def pick(x, index):
    half = x.shape[0] // 2
    return jnp.where(index == 1, x[half:], x[:half])


def params(mib):
    return pltpu.CompilerParams(vmem_limit_bytes=mib * MIB)


def whole():
    return pl.BlockSpec(memory_space=pltpu.VMEM)


def in_hbm(x):
    return pltpu.with_memory_space_constraint(x, pltpu.HBM)


def scalar():
    return pl.BlockSpec(memory_space=pltpu.SMEM)


MIX_CHUNKS = 2


def mix_kernel(start_ref, q_hbm, g_hbm, e_hbm, mixed_hbm, left_ref, q_ref, g_ref, e_ref, mixed_ref, wide_ref, q_sem, sems, out_sems):
    m_count, pack, rows, width = mixed_ref.shape
    rank = q_ref.shape[1]
    block = rows // MIX_CHUNKS
    q_copy = pltpu.make_async_copy(q_hbm, q_ref, q_sem)
    q_copy.start()
    start = start_ref[0]

    def copies(c):
        source = pl.ds(pl.multiple_of(start * rows + c * block, block), block)
        where = pl.ds(c * block, block)
        return [
            pltpu.make_async_copy(hbm.at[:, :, source, :], ref.at[:, :, where, :], sems.at[k, c])
            for k, (hbm, ref) in enumerate(((g_hbm, g_ref), (e_hbm, e_ref)))
        ]

    for c in range(MIX_CHUNKS):
        for copy in copies(c):
            copy.start()
    lane_group = lax.broadcasted_iota(jnp.int32, (width, LANES), 1) // rank
    q_copy.wait()
    for m in range(m_count):
        turned = jnp.concatenate([q_ref[m]] * pack, axis=0).T
        for j in range(pack):
            wide_ref[m, pl.ds(j * width, width), :] = jnp.where(lane_group == j, turned, 0.0).astype(BF16)
    outgoing = []
    for c in range(MIX_CHUNKS):
        for copy in copies(c):
            copy.wait()
        where = pl.ds(c * block, block)
        for m in range(m_count):
            parts = []
            for j in range(pack):
                mixed = g_ref[m, j, where, :] + e_ref[m, j, where, :]
                mixed_ref[m, j, where, :] = mixed
                parts.append(mixed)
            total = jnp.dot(jnp.concatenate(parts, axis=1), wide_ref[m], preferred_element_type=F32)
            left_ref[where, m * LANES:(m + 1) * LANES] = total.astype(left_ref.dtype)
        copy = pltpu.make_async_copy(mixed_ref.at[:, :, where, :], mixed_hbm.at[:, :, where, :], out_sems.at[c])
        copy.start()
        outgoing.append(copy)
    for copy in outgoing:
        copy.wait()


def mix(gradient, error_acc, q_turned, start, rows, dtype):
    m_count, pack, _, width = gradient.shape
    elements = m_count * pack * rows * width
    shape = (m_count, pack, rows, width)
    return pl.pallas_call(
        mix_kernel,
        in_specs=[scalar()] + [pl.BlockSpec(memory_space=pltpu.HBM)] * 3,
        out_specs=[pl.BlockSpec(memory_space=pltpu.HBM), whole()],
        out_shape=[pltpu.HBM(shape, BF16), pltpu.VMEM((rows, m_count * LANES), dtype)],
        scratch_shapes=[
            pltpu.VMEM(q_turned.shape, F32),
            pltpu.VMEM(shape, BF16),
            pltpu.VMEM(shape, BF16),
            pltpu.VMEM(shape, BF16),
            pltpu.VMEM((m_count, pack * width, LANES), BF16),
            pltpu.SemaphoreType.DMA,
            pltpu.SemaphoreType.DMA((2, MIX_CHUNKS)),
            pltpu.SemaphoreType.DMA((MIX_CHUNKS,)),
        ],
        compiler_params=params(16),
        cost_estimate=pl.CostEstimate(flops=2 * elements * LANES, bytes_accessed=4 * elements, transcendentals=0),
        name="mix",
    )(start.astype(jnp.int32).reshape(1), q_turned, gradient, error_acc)


def project_kernel(left_ref, mixed_ref, *refs):
    right_ref, gram_ref = refs[-2:]
    m_count, pack, _, width = mixed_ref.shape
    rank = LANES // pack
    left = left_ref[...]
    turned = left.T
    every = jnp.dot(turned, left, preferred_element_type=F32)
    for m in range(m_count):
        gram = jnp.zeros((rank, rank), F32)
        right = refs[0][m] if len(refs) == 3 else jnp.zeros((rank, width), F32)
        for j in range(pack):
            at = m * LANES + j * rank
            gram += every[at:at + rank, at:at + rank]
            right += jnp.dot(turned[at:at + rank], mixed_ref[m, j], preferred_element_type=F32)
        gram_ref[m] = gram
        right_ref[m] = right


def project(left, mixed, *before):
    m_count, pack, rows, width = mixed.shape
    rank = LANES // pack
    elements = m_count * pack * rows * width
    mixed = pltpu.with_memory_space_constraint(mixed, pltpu.VMEM)
    return pl.pallas_call(
        project_kernel,
        in_specs=[whole()] * (2 + len(before)),
        out_specs=[whole()] * 2,
        out_shape=[pltpu.VMEM((m_count, rank, width), F32), pltpu.VMEM((m_count, rank, rank), F32)],
        compiler_params=params(8),
        cost_estimate=pl.CostEstimate(flops=2 * elements * LANES * 4, bytes_accessed=0, transcendentals=0),
        name="project",
    )(left, mixed, *before)


def invert_kernel(steps, *refs):
    grams, held_ref = refs[:-1], refs[-1]
    m_count, rank, _ = held_ref.shape
    row_at = lax.broadcasted_iota(jnp.int32, (rank, rank), 0)
    col_at = lax.broadcasted_iota(jnp.int32, (rank, rank), 1)
    held = [grams[0][m] for m in range(m_count)]
    if len(grams) == 4:
        held = [(grams[0][m] + grams[1][m]) + (grams[2][m] + grams[3][m]) for m in range(m_count)]
    for k in steps:
        for m in range(m_count):
            a = held[m]
            row, col = a[k:k + 1, :], a[:, k:k + 1]
            inv = 1.0 / a[k:k + 1, k:k + 1]
            scaled = row * inv
            rest = a - col * scaled
            rest = jnp.where(row_at == k, scaled, rest)
            held[m] = jnp.where(col_at == k, jnp.where(row_at == k, inv, -col * inv), rest)
    for m in range(m_count):
        held_ref[m] = held[m]


def invert(steps, *grams):
    return pl.pallas_call(
        lambda *refs: invert_kernel(steps, *refs),
        in_specs=[whole()] * len(grams),
        out_specs=whole(),
        out_shape=pltpu.VMEM(grams[0].shape, F32),
        compiler_params=params(4),
        cost_estimate=pl.CostEstimate(flops=2 * 10**9, bytes_accessed=0, transcendentals=0),
        name="invert",
    )(*grams)


def expand_kernel(scale, place_ref, left_ref, inverse_ref, right_ref, update_ref, wide_ref, held_ref, sems):
    m_count, rank, width = right_ref.shape
    pack = LANES // rank
    count, block, _ = left_ref.shape
    wide_ref[...] = jnp.zeros_like(wide_ref)
    copies = []
    for m in range(m_count):
        z = jnp.dot(inverse_ref[m], right_ref[m], precision=lax.Precision.HIGHEST, preferred_element_type=F32) * scale
        high = z.astype(BF16)
        low = (z - high.astype(F32)).astype(BF16)
        for j in range(pack):
            wide_ref[m, j, pl.ds(j * rank, rank), :] = high
            wide_ref[m, j, pl.ds(LANES + j * rank, rank), :] = low
            for p in range(count):
                left = left_ref[p, :, m * LANES:(m + 1) * LANES]
                rows = jnp.dot(jnp.concatenate([left, left], axis=1), wide_ref[m, j], preferred_element_type=F32)
                held_ref[m, j, p] = rows.astype(BF16)
                where = pl.ds(pl.multiple_of(place_ref[p] * block, block), block)
                copy = pltpu.make_async_copy(held_ref.at[m, j, p], update_ref.at[m, j, where, :], sems.at[m, j, p])
                copy.start()
                copies.append(copy)
    for copy in copies:
        copy.wait()


def expand(pieces, places, inverse, right, scale):
    m_count, rank, width = right.shape
    pack = LANES // rank
    count, block, _ = pieces.shape
    out = pl.pallas_call(
        lambda *refs: expand_kernel(scale, *refs),
        in_specs=[scalar(), whole(), whole(), whole()],
        out_specs=pl.BlockSpec(memory_space=pl.ANY),
        out_shape=jax.ShapeDtypeStruct((m_count, pack, count * block, width), BF16),
        scratch_shapes=[
            pltpu.VMEM((m_count, pack, 2 * LANES, width), BF16),
            pltpu.VMEM((m_count, pack, count, block, width), BF16),
            pltpu.SemaphoreType.DMA((m_count, pack, count)),
        ],
        compiler_params=params(20),
        name="expand",
    )(places, pieces, inverse, right)
    return out.reshape(m_count, pack * count * block, width)


def sum_right(right, grams):
    outer, hst, _ = sizes()
    rank = right.shape[1]
    for b in range(bits(hst)):
        right = right + exchange(right, lambda o, h, t, b=b: (o, h ^ (1 << b), t))
    right, grams = lax.optimization_barrier((right, grams))
    inverse = invert(range(rank // 2), *grams)
    for b in range(bits(outer)):
        right = right + exchange(right, lambda o, h, t, b=b: (o ^ (1 << b), h, t))
        if b == 0:
            right, inverse = lax.optimization_barrier((right, inverse))
    return right, invert(range(rank // 2, rank), inverse)


def shards(gradient, error_acc, q_start):
    _, m_count, depth, width = gradient.shape
    rows = depth // PACK
    quarter = rows // 4
    shape = (m_count, PACK, rows, width)
    gradient, error_acc = in_hbm(gradient.reshape(shape)), in_hbm(error_acc.reshape(shape))
    q_turned = in_hbm(jnp.swapaxes(q_start, 1, 2))
    steps = replica_steps()
    o, h = lax.axis_index("outer"), lax.axis_index("hst")
    (partner0, bit0), (partner1, bit1) = steps[:2]
    b0, b1, beyond = bit0(o, h), bit1(o, h), bit1(o, h ^ 1)
    at_own, at_side = 2 * b0 + b1, 2 * b0 + 1 - b1
    at_far, at_far_side = 2 * (1 - b0) + beyond, 2 * (1 - b0) + 1 - beyond

    def mixed_left(at, dtype):
        return mix(gradient, error_acc, q_turned, at, quarter, dtype)

    mixed_far_side, left_far_side = mixed_left(at_far_side, BF16)
    came_side = exchange(left_far_side, partner0)
    mixed_side, left_side = mixed_left(at_side, F32)
    sent, at_far_late = lax.optimization_barrier(((left_side + came_side.astype(F32)).astype(BF16), at_far))
    side = exchange(sent, partner1)
    mixed_far, left_far = mixed_left(at_far_late, BF16)
    came_own = exchange(left_far, partner0)
    mixed_own, left = mixed_left(at_own, F32)
    left = left + came_own.astype(F32) + side.astype(F32)
    for partner, bit in steps[2:]:
        b = bit(o, h)
        left = pick(left, b) + exchange(pick(left, 1 - b).astype(BF16), partner).astype(F32)
    for b in range(bits(lax.axis_size("tp"))):
        sent = left.astype(BF16)
        left = sent.astype(F32) + exchange(sent, lambda o, h, t, b=b: (o, h, t ^ (1 << b))).astype(F32)
    own = left.astype(BF16)

    for partner, bit in reversed(steps[2:]):
        b = bit(o, h)
        other = exchange(own, partner)
        own = jnp.concatenate([jnp.where(b == 1, other, own), jnp.where(b == 1, own, other)])
    far = exchange(own, partner0)
    side = exchange(own, partner1)
    right, gram_own = project(own, mixed_own)
    right, gram_far = project(far, mixed_far, right)
    side, right = lax.optimization_barrier((side, right))
    far_side = exchange(side, partner0)
    right, gram_side = project(side, mixed_side, right)
    right, gram_far_side = project(far_side, mixed_far_side, right)

    near, beyond = (gram_own, gram_side), (gram_far, gram_far_side)
    right, inverse = sum_right(right, near + beyond)
    outer, hst, _ = sizes()
    pieces = jnp.stack([own, far, side, far_side])
    places = jnp.stack([at_own, at_far, at_side, at_far_side]).astype(jnp.int32)
    return expand(pieces, places, inverse, right, 1.0 / (outer * hst))


def solution(mesh):
    in_specs = (
        P(("outer", "hst"), None, None, "tp"),
        P(("outer", "hst"), None, None, "tp"),
        P(None, "tp", None),
    )
    out_specs = P(None, None, "tp")
    return jax.shard_map(shards, mesh=mesh, in_specs=in_specs, out_specs=out_specs, check_vma=False)
```

```python
import jax
import jax.numpy as jnp
from jax import lax
from jax.experimental import pallas as pl
from jax.experimental.pallas import tpu as pltpu
from jax.sharding import PartitionSpec as P

AXES = ("outer", "hst", "tp")
PACK = 4
LANES = 128
F32, BF16 = jnp.float32, jnp.bfloat16
MIB = 1024 * 1024


def bits(size):
    return size.bit_length() - 1


def sizes():
    return tuple(lax.axis_size(axis) for axis in AXES)


def coordinates(index):
    _, hst, tp = sizes()
    return index // (hst * tp), index // tp % hst, index % tp


def exchange(x, partner):
    _, hst, tp = sizes()
    pairs = []
    for index in range(sizes()[0] * hst * tp):
        o, h, t = partner(*coordinates(index))
        pairs.append((index, (o * hst + h) * tp + t))
    return lax.ppermute(x, AXES, pairs)


def replica_steps():
    outer, hst, _ = sizes()
    steps = []
    for b in range(bits(hst)):
        steps.append((lambda o, h, t, b=b: (o, h ^ (1 << b), t), lambda o, h, b=b: (h >> b) & 1))
    n = bits(outer)
    for b in range(n):
        def partner(o, h, t, b=b):
            return o ^ (1 << (b if h % 2 == 0 else n - 1 - b)), h, t

        def bit(o, h, b=b):
            return jnp.where(h % 2 == 0, (o >> b) & 1, (o >> (n - 1 - b)) & 1)

        steps.append((partner, bit))
    return steps


def pick(x, index):
    half = x.shape[0] // 2
    return jnp.where(index == 1, x[half:], x[:half])


def params(mib):
    return pltpu.CompilerParams(vmem_limit_bytes=mib * MIB)


def cost():
    return pl.CostEstimate(flops=10**6, bytes_accessed=0, transcendentals=0)


def whole():
    return pl.BlockSpec(memory_space=pltpu.VMEM)


def in_hbm(x):
    return pltpu.with_memory_space_constraint(x, pltpu.HBM)


def scalar():
    return pl.BlockSpec(memory_space=pltpu.SMEM)


MIX_CHUNK, KEEP_CHUNK = 512, 256


def load(starts, chunk, g_hbm, e_hbm, g_ref, e_ref, sems):
    chunks = []
    for c, start in enumerate(starts):
        source = pl.ds(pl.multiple_of(start, chunk), chunk)
        where = pl.ds(c * chunk, chunk)
        copies = [
            pltpu.make_async_copy(hbm.at[:, :, source, :], ref.at[:, :, where, :], sems.at[k, c])
            for k, (hbm, ref) in enumerate(((g_hbm, g_ref), (e_hbm, e_ref)))
        ]
        for copy in copies:
            copy.start()
        chunks.append((where, copies))
    return chunks


def mix_kernel(place_ref, q_hbm, g_hbm, e_hbm, first_ref, second_ref, q_ref, g_ref, e_ref, wide_ref, q_sem, sems):
    m_count, pack, _, width = g_ref.shape
    rank = q_ref.shape[1]
    rows = first_ref.shape[0]
    outs = (first_ref, second_ref)
    starts = [place_ref[k] * rows + c * MIX_CHUNK for k in range(2) for c in range(rows // MIX_CHUNK)]
    q_copy = pltpu.make_async_copy(q_hbm, q_ref, q_sem)
    q_copy.start()
    chunks = load(starts, MIX_CHUNK, g_hbm, e_hbm, g_ref, e_ref, sems)
    lane_group = lax.broadcasted_iota(jnp.int32, (width, LANES), 1) // rank
    q_copy.wait()
    for m in range(m_count):
        turned = jnp.concatenate([q_ref[m]] * pack, axis=0).T
        for j in range(pack):
            wide_ref[m, pl.ds(j * width, width), :] = jnp.where(lane_group == j, turned, 0.0).astype(BF16)
    for c, (where, copies) in enumerate(chunks):
        for copy in copies:
            copy.wait()
        left_ref = outs[c * MIX_CHUNK // rows]
        for m in range(m_count):
            mixed = [g_ref[m, j, where, :] + e_ref[m, j, where, :] for j in range(pack)]
            total = jnp.dot(jnp.concatenate(mixed, axis=1), wide_ref[m], preferred_element_type=F32)
            left_ref[pl.ds(c * MIX_CHUNK % rows, MIX_CHUNK), m * LANES:(m + 1) * LANES] = total.astype(left_ref.dtype)


def mix(gradient, error_acc, q_turned, first, second, rows):
    m_count, pack, _, width = gradient.shape
    shape = (m_count, pack, 2 * rows, width)
    return pl.pallas_call(
        mix_kernel,
        in_specs=[scalar()] + [pl.BlockSpec(memory_space=pltpu.HBM)] * 3,
        out_specs=[whole()] * 2,
        out_shape=[pltpu.VMEM((rows, m_count * LANES), dtype) for dtype in (BF16, F32)],
        scratch_shapes=[
            pltpu.VMEM(q_turned.shape, F32),
            pltpu.VMEM(shape, BF16),
            pltpu.VMEM(shape, BF16),
            pltpu.VMEM((m_count, pack * width, LANES), BF16),
            pltpu.SemaphoreType.DMA,
            pltpu.SemaphoreType.DMA((2, 2 * rows // MIX_CHUNK)),
        ],
        compiler_params=params(16),
        cost_estimate=cost(),
        name="mix",
    )(jnp.stack([first, second]).astype(jnp.int32), q_turned, gradient, error_acc)


def keep_kernel(place_ref, g_hbm, e_hbm, mixed_hbm, g_ref, e_ref, sems, out_sems):
    rows = g_ref.shape[2]
    starts = [place_ref[0] * rows + c * KEEP_CHUNK for c in range(rows // KEEP_CHUNK)]
    outgoing = []
    for c, (where, copies) in enumerate(load(starts, KEEP_CHUNK, g_hbm, e_hbm, g_ref, e_ref, sems)):
        for copy in copies:
            copy.wait()
        g_ref[:, :, where, :] = g_ref[:, :, where, :] + e_ref[:, :, where, :]
        copy = pltpu.make_async_copy(g_ref.at[:, :, where, :], mixed_hbm.at[:, :, where, :], out_sems.at[c])
        copy.start()
        outgoing.append(copy)
    for copy in outgoing:
        copy.wait()


def keep(gradient, error_acc, place, rows):
    m_count, pack, _, width = gradient.shape
    shape = (m_count, pack, rows, width)
    return pl.pallas_call(
        keep_kernel,
        in_specs=[scalar()] + [pl.BlockSpec(memory_space=pltpu.HBM)] * 2,
        out_specs=pl.BlockSpec(memory_space=pltpu.HBM),
        out_shape=pltpu.HBM(shape, BF16),
        scratch_shapes=[
            pltpu.VMEM(shape, BF16),
            pltpu.VMEM(shape, BF16),
            pltpu.SemaphoreType.DMA((2, rows // KEEP_CHUNK)),
            pltpu.SemaphoreType.DMA((rows // KEEP_CHUNK,)),
        ],
        compiler_params=params(12),
        cost_estimate=cost(),
        name="keep",
    )(place.astype(jnp.int32).reshape(1), gradient, error_acc)


def project_kernel(left_ref, mixed_ref, *refs):
    right_ref, gram_ref = refs[-2:]
    m_count, pack, _, width = mixed_ref.shape
    rank = LANES // pack
    left = left_ref[...]
    turned = left.T
    every = jnp.dot(turned, left, preferred_element_type=F32)
    for m in range(m_count):
        gram = jnp.zeros((rank, rank), F32)
        right = refs[0][m] if len(refs) == 3 else jnp.zeros((rank, width), F32)
        for j in range(pack):
            at = m * LANES + j * rank
            gram += every[at:at + rank, at:at + rank]
            right += jnp.dot(turned[at:at + rank], mixed_ref[m, j], preferred_element_type=F32)
        gram_ref[m] = gram
        right_ref[m] = right


def project(left, mixed, *before):
    m_count, pack, rows, width = mixed.shape
    rank = LANES // pack
    mixed = pltpu.with_memory_space_constraint(mixed, pltpu.VMEM)
    return pl.pallas_call(
        project_kernel,
        in_specs=[whole()] * (2 + len(before)),
        out_specs=[whole()] * 2,
        out_shape=[pltpu.VMEM((m_count, rank, width), F32), pltpu.VMEM((m_count, rank, rank), F32)],
        compiler_params=params(8),
        cost_estimate=cost(),
        name="project",
    )(left, mixed, *before)


def invert_kernel(steps, *refs):
    grams, held_ref = refs[:-1], refs[-1]
    m_count, rank, _ = held_ref.shape
    row_at = lax.broadcasted_iota(jnp.int32, (rank, rank), 0)
    col_at = lax.broadcasted_iota(jnp.int32, (rank, rank), 1)
    held = [grams[0][m] for m in range(m_count)]
    if len(grams) == 4:
        held = [(grams[0][m] + grams[1][m]) + (grams[2][m] + grams[3][m]) for m in range(m_count)]
    for k in steps:
        for m in range(m_count):
            a = held[m]
            row, col = a[k:k + 1, :], a[:, k:k + 1]
            inv = 1.0 / a[k:k + 1, k:k + 1]
            scaled = row * inv
            rest = a - col * scaled
            rest = jnp.where(row_at == k, scaled, rest)
            held[m] = jnp.where(col_at == k, jnp.where(row_at == k, inv, -col * inv), rest)
    for m in range(m_count):
        held_ref[m] = held[m]


def invert(steps, *grams):
    return pl.pallas_call(
        lambda *refs: invert_kernel(steps, *refs),
        in_specs=[whole()] * len(grams),
        out_specs=whole(),
        out_shape=pltpu.VMEM(grams[0].shape, F32),
        compiler_params=params(4),
        cost_estimate=cost(),
        name="invert",
    )(*grams)


def three_parts(x):
    high = x.astype(BF16)
    rest = x - high.astype(F32)
    middle = rest.astype(BF16)
    return high, middle, (rest - middle.astype(F32)).astype(BF16)


def small_dot(a, b):
    a0, a1, a2 = three_parts(a)
    b0, b1, b2 = three_parts(b)
    wide = jnp.concatenate([a0, a0, a1, a1, a0, a2], axis=1)
    tall = jnp.concatenate([b0, b1, b0, b1, b2, b0], axis=0)
    return jnp.dot(wide, tall, preferred_element_type=F32)


def expand_kernel(scale, place_ref, left_ref, inverse_ref, right_ref, update_ref, wide_ref, held_ref, sems):
    m_count, rank, width = right_ref.shape
    pack = LANES // rank
    count, block, _ = left_ref.shape
    wide_ref[...] = jnp.zeros_like(wide_ref)
    copies = []
    for m in range(m_count):
        z = small_dot(inverse_ref[m], right_ref[m]) * scale
        high = z.astype(BF16)
        low = (z - high.astype(F32)).astype(BF16)
        for j in range(pack):
            wide_ref[m, j, pl.ds(j * rank, rank), :] = high
            wide_ref[m, j, pl.ds(LANES + j * rank, rank), :] = low
            for p in range(count):
                left = left_ref[p, :, m * LANES:(m + 1) * LANES]
                rows = jnp.dot(jnp.concatenate([left, left], axis=1), wide_ref[m, j], preferred_element_type=F32)
                held_ref[m, j, p] = rows.astype(BF16)
                where = pl.ds(pl.multiple_of(place_ref[p] * block, block), block)
                copy = pltpu.make_async_copy(held_ref.at[m, j, p], update_ref.at[m, j, where, :], sems.at[m, j, p])
                copy.start()
                copies.append(copy)
    for copy in copies:
        copy.wait()


def expand(pieces, places, inverse, right, scale):
    m_count, rank, width = right.shape
    pack = LANES // rank
    count, block, _ = pieces.shape
    out = pl.pallas_call(
        lambda *refs: expand_kernel(scale, *refs),
        in_specs=[scalar(), whole(), whole(), whole()],
        out_specs=pl.BlockSpec(memory_space=pl.ANY),
        out_shape=jax.ShapeDtypeStruct((m_count, pack, count * block, width), BF16),
        scratch_shapes=[
            pltpu.VMEM((m_count, pack, 2 * LANES, width), BF16),
            pltpu.VMEM((m_count, pack, count, block, width), BF16),
            pltpu.SemaphoreType.DMA((m_count, pack, count)),
        ],
        compiler_params=params(20),
        name="expand",
    )(places, pieces, inverse, right)
    return out.reshape(m_count, pack * count * block, width)


def sum_right(right, grams):
    outer, hst, _ = sizes()
    rank = right.shape[1]
    for b in range(bits(hst)):
        right = right + exchange(right, lambda o, h, t, b=b: (o, h ^ (1 << b), t))
    early = rank * 3 // 8
    right, inverse = after(right, invert(range(early), *grams))
    parts = [right] + [exchange(right, lambda o, h, t, k=k: (o ^ k, h, t)) for k in range(1, outer)]
    inverse = invert(range(early, rank), inverse)
    while len(parts) > 1:
        parts = [parts[k] + parts[k + 1] for k in range(0, len(parts), 2)]
    return parts[0], inverse


def after(value, *others):
    return lax.optimization_barrier((value, *others))


def shards(gradient, error_acc, q_start):
    _, m_count, depth, width = gradient.shape
    rows = depth // PACK
    quarter = rows // 4
    shape = (m_count, PACK, rows, width)
    gradient, error_acc = in_hbm(gradient.reshape(shape)), in_hbm(error_acc.reshape(shape))
    q_turned = in_hbm(jnp.swapaxes(q_start, 1, 2))
    steps = replica_steps()
    o, h = lax.axis_index("outer"), lax.axis_index("hst")
    (partner0, bit0), (partner1, bit1) = steps[:2]
    b0, b1, beyond = bit0(o, h), bit1(o, h), bit1(o, h ^ 1)
    at_own, at_side = 2 * b0 + b1, 2 * b0 + 1 - b1
    at_far, at_far_side = 2 * (1 - b0) + beyond, 2 * (1 - b0) + 1 - beyond
    waiting, mixed = [at_own, at_far, at_side, at_far_side], []

    def swap(x, partner):
        if not waiting:
            return exchange(x, partner)
        x, at = after(x, waiting.pop(0))
        kept = keep(gradient, error_acc, at, quarter)
        came, kept = after(exchange(x, partner), kept)
        mixed.append(kept)
        return came

    left_far_side, left = mix(gradient, error_acc, q_turned, at_far_side, at_side, quarter)
    left = left + exchange(left_far_side, partner0).astype(F32)
    sent, at = after(left.astype(BF16), at_far)
    side = exchange(sent, partner1)
    left_far, left = mix(gradient, error_acc, q_turned, at, at_own, quarter)
    left = left + exchange(left_far, partner0).astype(F32) + side.astype(F32)
    for partner, bit in steps[2:]:
        b = bit(o, h)
        left = pick(left, b) + swap(pick(left, 1 - b).astype(BF16), partner).astype(F32)
    for b in range(bits(lax.axis_size("tp"))):
        sent = left.astype(BF16)
        left = sent.astype(F32) + swap(sent, lambda o, h, t, b=b: (o, h, t ^ (1 << b))).astype(F32)
    own = left.astype(BF16)

    for partner, bit in reversed(steps[2:]):
        b = bit(o, h)
        other = swap(own, partner)
        own = jnp.concatenate([jnp.where(b == 1, other, own), jnp.where(b == 1, own, other)])
    far = exchange(own, partner0)
    side = exchange(own, partner1)
    right, gram_own = project(own, mixed[0])
    right, gram_far = project(far, mixed[1], right)
    side, right = after(side, right)
    far_side = exchange(side, partner0)
    right, gram_side = project(side, mixed[2], right)
    right, gram_far_side = project(far_side, mixed[3], right)

    right, inverse = sum_right(right, (gram_own, gram_side, gram_far, gram_far_side))
    outer, hst, _ = sizes()
    pieces = jnp.stack([own, far, side, far_side])
    places = jnp.stack([at_own, at_far, at_side, at_far_side]).astype(jnp.int32)
    return expand(pieces, places, inverse, right, 1.0 / (outer * hst))


def solution(mesh):
    in_specs = (
        P(("outer", "hst"), None, None, "tp"),
        P(("outer", "hst"), None, None, "tp"),
        P(None, "tp", None),
    )
    out_specs = P(None, None, "tp")
    return jax.shard_map(shards, mesh=mesh, in_specs=in_specs, out_specs=out_specs, check_vma=False)
```

```python
import jax
import jax.numpy as jnp
from jax import lax
from jax.experimental import pallas as pl
from jax.experimental.pallas import tpu as pltpu
from jax.sharding import PartitionSpec as P

AXES = ("outer", "hst", "tp")
PACK = 4
LANES = 128
F32, BF16 = jnp.float32, jnp.bfloat16
MIB = 1024 * 1024


def bits(size):
    return size.bit_length() - 1


def sizes():
    return tuple(lax.axis_size(axis) for axis in AXES)


def coordinates(index):
    _, hst, tp = sizes()
    return index // (hst * tp), index // tp % hst, index % tp


def exchange(x, partner):
    _, hst, tp = sizes()
    pairs = []
    for index in range(sizes()[0] * hst * tp):
        o, h, t = partner(*coordinates(index))
        pairs.append((index, (o * hst + h) * tp + t))
    return lax.ppermute(x, AXES, pairs)


def pick(x, index):
    half = x.shape[0] // 2
    return jnp.where(index == 1, x[half:], x[:half])


def params(mib):
    return pltpu.CompilerParams(vmem_limit_bytes=mib * MIB)


def cost():
    return pl.CostEstimate(flops=10**6, bytes_accessed=0, transcendentals=0)


def whole():
    return pl.BlockSpec(memory_space=pltpu.VMEM)


def in_hbm(x):
    return pltpu.with_memory_space_constraint(x, pltpu.HBM)


def scalar():
    return pl.BlockSpec(memory_space=pltpu.SMEM)


def load(starts, rows, g_hbm, e_hbm, g_ref, e_ref, sems):
    chunks = []
    for c, start in enumerate(starts):
        source = pl.ds(pl.multiple_of(start, rows), rows)
        where = pl.ds(c * rows, rows)
        copies = [
            pltpu.make_async_copy(hbm.at[:, :, source, :], ref.at[:, :, where, :], sems.at[k, c])
            for k, (hbm, ref) in enumerate(((g_hbm, g_ref), (e_hbm, e_ref)))
        ]
        chunks.append((where, copies))
    return chunks


def start_all(copies):
    for k, copy in enumerate(copies):
        copy.start(priority=1)


def wait_all(copies):
    for copy in copies:
        copy.wait()


FETCHES = 4


def mix_kernel(place_ref, q_hbm, g_hbm, e_hbm, *refs):
    mixed_hbm = refs[2] if len(refs) == 10 else None
    first_ref, second_ref = refs[:2]
    q_ref, g_ref, e_ref, wide_ref, q_sem, sems, out_sems = refs[-7:]
    m_count, pack, total_rows, width = g_ref.shape
    rank = q_ref.shape[1]
    count = place_ref.shape[0]
    rows = total_rows // count
    q_copy = pltpu.make_async_copy(q_hbm, q_ref, q_sem)
    q_copy.start()
    chunks = load([place_ref[c] * rows for c in range(count)], rows, g_hbm, e_hbm, g_ref, e_ref, sems)
    for _, copies in chunks[:FETCHES]:
        start_all(copies)
    lane_group = lax.broadcasted_iota(jnp.int32, (width, LANES), 1) // rank
    q_copy.wait()
    for m in range(m_count):
        turned = jnp.concatenate([q_ref[m]] * pack, axis=0).T
        for j in range(pack):
            wide_ref[m, pl.ds(j * width, width), :] = jnp.where(lane_group == j, turned, 0.0).astype(BF16)
    outgoing = []
    for c, (where, copies) in enumerate(chunks):
        wait_all(copies)
        if c + FETCHES < count:
            start_all(chunks[c + FETCHES][1])
        left_ref = first_ref if c < count // 2 else second_ref
        at = pl.ds(c % (count // 2) * rows, rows)
        for m in range(m_count):
            mixed = [g_ref[m, j, where, :] + e_ref[m, j, where, :] for j in range(pack)]
            total = jnp.dot(jnp.concatenate(mixed, axis=1), wide_ref[m], preferred_element_type=F32)
            left_ref[at, m * LANES:(m + 1) * LANES] = total.astype(left_ref.dtype)
            if mixed_hbm is not None:
                for j in range(pack):
                    g_ref[m, j, where, :] = mixed[j]
        if mixed_hbm is not None:
            copy = pltpu.make_async_copy(g_ref.at[:, :, where, :], mixed_hbm.at[:, :, where, :], out_sems.at[c])
            copy.start()
            outgoing.append(copy)
    wait_all(outgoing)


def mix(gradient, error_acc, q_turned, first, second, rows, kept=False):
    m_count, pack, _, width = gradient.shape
    places = jnp.stack(first + second).astype(jnp.int32)
    count = len(first + second)
    shape = (m_count, pack, count * rows, width)
    hbm = pl.BlockSpec(memory_space=pltpu.HBM)
    return pl.pallas_call(
        mix_kernel,
        in_specs=[scalar()] + [hbm] * 3,
        out_specs=[whole()] * 2 + [hbm] * kept,
        out_shape=[pltpu.VMEM((len(first) * rows, m_count * LANES), dtype) for dtype in (BF16, F32)] + [pltpu.HBM(shape, BF16)] * kept,
        scratch_shapes=[
            pltpu.VMEM(q_turned.shape, F32),
            pltpu.VMEM(shape, BF16),
            pltpu.VMEM(shape, BF16),
            pltpu.VMEM((m_count, pack * width, LANES), BF16),
            pltpu.SemaphoreType.DMA,
            pltpu.SemaphoreType.DMA((2, count)),
            pltpu.SemaphoreType.DMA((count,)),
        ],
        compiler_params=params(20),
        cost_estimate=cost(),
        name="mix",
    )(places, q_turned, gradient, error_acc)


def keep_kernel(place_ref, g_hbm, e_hbm, mixed_hbm, g_ref, e_ref, sems, out_sems):
    count = place_ref.shape[0]
    rows = g_ref.shape[2] // count
    outgoing = []
    chunks = load([place_ref[c] * rows for c in range(count)], rows, g_hbm, e_hbm, g_ref, e_ref, sems)
    for _, copies in chunks:
        start_all(copies)
    for c, (where, copies) in enumerate(chunks):
        wait_all(copies)
        g_ref[:, :, where, :] = g_ref[:, :, where, :] + e_ref[:, :, where, :]
        copy = pltpu.make_async_copy(g_ref.at[:, :, where, :], mixed_hbm.at[:, :, where, :], out_sems.at[c])
        copy.start()
        outgoing.append(copy)
    wait_all(outgoing)


def keep(gradient, error_acc, places, rows):
    m_count, pack, _, width = gradient.shape
    count = len(places)
    shape = (m_count, pack, count * rows, width)
    return pl.pallas_call(
        keep_kernel,
        in_specs=[scalar()] + [pl.BlockSpec(memory_space=pltpu.HBM)] * 2,
        out_specs=pl.BlockSpec(memory_space=pltpu.HBM),
        out_shape=pltpu.HBM(shape, BF16),
        scratch_shapes=[
            pltpu.VMEM(shape, BF16),
            pltpu.VMEM(shape, BF16),
            pltpu.SemaphoreType.DMA((2, count)),
            pltpu.SemaphoreType.DMA((count,)),
        ],
        compiler_params=params(16),
        cost_estimate=cost(),
        name="keep",
    )(jnp.stack(places).astype(jnp.int32), gradient, error_acc)


def project_kernel(chunks, *refs):
    count = len(chunks)
    lefts, right_ref, gram_ref = refs[:count], refs[-2], refs[-1]
    stores = 1 + max(store for store, _ in chunks)
    mixed = refs[count:count + stores]
    before = refs[count + stores:-2]
    m_count, pack, _, width = mixed[0].shape
    rank = LANES // pack
    right = [before[0][m] if before else jnp.zeros((rank, width), F32) for m in range(m_count)]
    for c, (store, place) in enumerate(chunks):
        left = lefts[c][...]
        rows = left.shape[0]
        turned = left.T
        every = jnp.dot(turned, left, preferred_element_type=F32)
        for m in range(m_count):
            gram = jnp.zeros((rank, rank), F32)
            for j in range(pack):
                at = m * LANES + j * rank
                gram += every[at:at + rank, at:at + rank]
                block = mixed[store][m, j, pl.ds(place * rows, rows), :]
                right[m] += jnp.dot(turned[at:at + rank], block, preferred_element_type=F32)
            gram_ref[c, m] = gram
    for m in range(m_count):
        right_ref[m] = right[m]


def project(lefts, mixed, chunks, *before):
    m_count, pack, _, width = mixed[0].shape
    rank = LANES // pack
    mixed = [pltpu.with_memory_space_constraint(x, pltpu.VMEM) for x in mixed]
    return pl.pallas_call(
        lambda *refs: project_kernel(chunks, *refs),
        in_specs=[whole()] * (len(lefts) + len(mixed) + len(before)),
        out_specs=[whole()] * 2,
        out_shape=[pltpu.VMEM((m_count, rank, width), F32), pltpu.VMEM((len(lefts), m_count, rank, rank), F32)],
        compiler_params=params(8),
        cost_estimate=cost(),
        name="project",
    )(*lefts, *mixed, *before)


def tree_sum(parts):
    while len(parts) > 1:
        parts = [parts[k] + parts[k + 1] for k in range(0, len(parts), 2)]
    return parts[0]


def invert_kernel(steps, *refs):
    grams, held_ref = refs[:-1], refs[-1]
    m_count, rank, _ = held_ref.shape
    row_at = lax.broadcasted_iota(jnp.int32, (rank, rank), 0)
    col_at = lax.broadcasted_iota(jnp.int32, (rank, rank), 1)
    held = [grams[0][m] for m in range(m_count)] if len(grams) == 1 else [
        tree_sum([grams[0][0, m]] + [grams[1][c, m] for c in range(grams[1].shape[0])])
        + tree_sum([grams[0][1, m]] + [grams[2][c, m] for c in range(grams[2].shape[0])])
        for m in range(m_count)
    ]
    for k in steps:
        for m in range(m_count):
            a = held[m]
            row, col = a[k:k + 1, :], a[:, k:k + 1]
            inv = 1.0 / a[k:k + 1, k:k + 1]
            scaled = row * inv
            rest = a - col * scaled
            rest = jnp.where(row_at == k, scaled, rest)
            held[m] = jnp.where(col_at == k, jnp.where(row_at == k, inv, -col * inv), rest)
    for m in range(m_count):
        held_ref[m] = held[m]


def invert(steps, *grams):
    return pl.pallas_call(
        lambda *refs: invert_kernel(steps, *refs),
        in_specs=[whole()] * len(grams),
        out_specs=whole(),
        out_shape=pltpu.VMEM(grams[0].shape[-3:], F32),
        compiler_params=params(4),
        cost_estimate=cost(),
        name="invert",
    )(*grams)


def three_parts(x):
    high = x.astype(BF16)
    rest = x - high.astype(F32)
    middle = rest.astype(BF16)
    return high, middle, (rest - middle.astype(F32)).astype(BF16)


def small_dot(a, b):
    a0, a1, a2 = three_parts(a)
    b0, b1, b2 = three_parts(b)
    wide = jnp.concatenate([a0, a0, a1, a1, a0, a2], axis=1)
    tall = jnp.concatenate([b0, b1, b0, b1, b2, b0], axis=0)
    return jnp.dot(wide, tall, preferred_element_type=F32)


def expand_kernel(scale, place_ref, left_ref, inverse_ref, right_ref, update_ref, wide_ref, held_ref, sems):
    m_count, rank, width = right_ref.shape
    pack = LANES // rank
    count, block, _ = left_ref.shape
    wide_ref[...] = jnp.zeros_like(wide_ref)
    copies = []
    for m in range(m_count):
        z = small_dot(inverse_ref[m], right_ref[m]) * scale
        high = z.astype(BF16)
        low = (z - high.astype(F32)).astype(BF16)
        for j in range(pack):
            wide_ref[m, j, pl.ds(j * rank, rank), :] = high
            wide_ref[m, j, pl.ds(LANES + j * rank, rank), :] = low
            for p in range(count):
                left = left_ref[p, :, m * LANES:(m + 1) * LANES]
                rows = jnp.dot(jnp.concatenate([left, left], axis=1), wide_ref[m, j], preferred_element_type=F32)
                held_ref[m, j, p] = rows.astype(BF16)
                where = pl.ds(pl.multiple_of(place_ref[p] * block, block), block)
                copy = pltpu.make_async_copy(held_ref.at[m, j, p], update_ref.at[m, j, where, :], sems.at[m, j, p])
                copy.start(priority=p % 2)
                copies.append(copy)
    for copy in copies:
        copy.wait()


def expand(pieces, places, inverse, right, scale):
    m_count, rank, width = right.shape
    pack = LANES // rank
    count, block, _ = pieces.shape
    out = pl.pallas_call(
        lambda *refs: expand_kernel(scale, *refs),
        in_specs=[scalar(), whole(), whole(), whole()],
        out_specs=pl.BlockSpec(memory_space=pl.ANY),
        out_shape=jax.ShapeDtypeStruct((m_count, pack, count * block, width), BF16),
        scratch_shapes=[
            pltpu.VMEM((m_count, pack, 2 * LANES, width), BF16),
            pltpu.VMEM((m_count, pack, count, block, width), BF16),
            pltpu.SemaphoreType.DMA((m_count, pack, count)),
        ],
        compiler_params=params(20),
        name="expand",
    )(places, pieces, inverse, right)
    return out.reshape(m_count, pack * count * block, width)


def sum_right(right, grams):
    outer, hst, _ = sizes()
    rank = right.shape[1]
    for b in range(bits(hst)):
        right = right + exchange(right, lambda o, h, t, b=b: (o, h ^ (1 << b), t))
    early = rank * 3 // 8
    right, inverse = after(right, invert(range(early), *grams))
    parts = [right] + [exchange(right, lambda o, h, t, k=k: (o ^ k, h, t)) for k in range(1, outer)]
    inverse = invert(range(early, rank), inverse)
    return tree_sum(parts), inverse


def after(value, *others):
    return lax.optimization_barrier((value, *others))


def shards(gradient, error_acc, q_start):
    _, m_count, depth, width = gradient.shape
    outer, hst, tp = sizes()
    rows = depth // PACK
    chunk = rows // (2 * outer)
    shape = (m_count, PACK, rows, width)
    gradient, error_acc = in_hbm(gradient.reshape(shape)), in_hbm(error_acc.reshape(shape))
    q_turned = in_hbm(jnp.swapaxes(q_start, 1, 2))
    o, h = lax.axis_index("outer"), lax.axis_index("hst")
    near = [(h & 1) * outer + (o ^ k) for k in range(outer)]
    far = [(1 - (h & 1)) * outer + (o ^ k) for k in range(outer)]

    def core(x):
        return exchange(x, lambda o, h, t: (o, h ^ 1, t))

    def chip(x, k):
        return exchange(x, lambda o, h, t: (o ^ k, h, t))

    def after_all(value, places):
        value, *places = after(value, *places)
        return value, places

    left_far, left = mix(gradient, error_acc, q_turned, far[1:], near[1:], chunk)
    sent = (left + core(left_far).astype(F32)).astype(BF16)
    sent, (at_far, at_near) = after_all(sent, [far[0], near[0]])
    came = [chip(sent[(k - 1) * chunk:k * chunk], k) for k in range(1, outer)]
    left_far, left, mixed_own = mix(gradient, error_acc, q_turned, [at_far], [at_near], chunk, True)
    left = left + core(left_far).astype(F32)
    for part in came:
        left = left + part.astype(F32)
    for b in range(1, bits(hst)):
        bit = (h >> b) & 1
        sent = pick(left, 1 - bit).astype(BF16)
        left = pick(left, bit) + exchange(sent, lambda o, h, t, b=b: (o, h ^ (1 << b), t)).astype(F32)
    others = near[1:] + far[1:]
    early, late = len(others) // 6, len(others) * 2 // 3
    waiting, mixed = [others[:early], others[early:late]], []
    for b in range(bits(tp)):
        sent = left.astype(BF16)
        places = waiting.pop(0) if waiting else None
        if places:
            sent, places = after_all(sent, places)
            kept = keep(gradient, error_acc, places, chunk)
        got = exchange(sent, lambda o, h, t, b=b: (o, h, t ^ (1 << b)))
        if places:
            got, kept = after(got, kept)
            mixed.append(kept)
        left = sent.astype(F32) + got.astype(F32)
    mixed += [keep(gradient, error_acc, places, chunk) for places in waiting]
    own = left.astype(BF16)

    for b in reversed(range(1, bits(hst))):
        bit = (h >> b) & 1
        got = exchange(own, lambda o, h, t, b=b: (o, h ^ (1 << b), t))
        own = jnp.concatenate([jnp.where(bit == 1, got, own), jnp.where(bit == 1, own, got)])
    own, places = after_all(own, others[late:])
    near_left, far_left = [own], [core(own)]
    came = [chip(own, k) for k in range(1, outer)]
    right, gram_own = project([own, far_left[0]], [mixed_own], [(0, 1), (0, 0)])
    mixed.append(keep(gradient, error_acc, places, chunk))
    came[-1], right, mixed[2] = after(came[-1], right, mixed[2])
    near_left += came
    far_left += [core(part) for part in came]
    where = [(0, k) for k in range(early)] + [(1, k) for k in range(late - early)] + [(2, k) for k in range(len(others) - late)]
    n = outer - 1

    def project_others(lefts, chunks, right):
        used = sorted({store for store, _ in chunks})
        chunks = [(used.index(store), place) for store, place in chunks]
        return project(lefts, [mixed[store] for store in used], chunks, right)

    right, gram_near = project_others(near_left[1:], where[:n], right)
    right, gram_far = project_others(far_left[1:], where[n:], right)

    right, inverse = sum_right(right, (gram_own, gram_near, gram_far))
    pieces = jnp.stack(near_left + far_left)
    places = jnp.stack(near + far).astype(jnp.int32)
    return expand(pieces, places, inverse, right, 1.0 / (outer * hst))


def solution(mesh):
    in_specs = (
        P(("outer", "hst"), None, None, "tp"),
        P(("outer", "hst"), None, None, "tp"),
        P(None, "tp", None),
    )
    out_specs = P(None, None, "tp")
    return jax.shard_map(shards, mesh=mesh, in_specs=in_specs, out_specs=out_specs, check_vma=False)
```

```python
import jax
import jax.numpy as jnp
from jax import lax
from jax.experimental import pallas as pl
from jax.experimental.pallas import tpu as pltpu
from jax.sharding import PartitionSpec as P

AXES = ("outer", "hst", "tp")
PACK = 4
LANES = 128
F32, BF16 = jnp.float32, jnp.bfloat16
MIB = 1024 * 1024


def bits(size):
    return size.bit_length() - 1


def sizes():
    return tuple(lax.axis_size(axis) for axis in AXES)


def coordinates(index):
    _, hst, tp = sizes()
    return index // (hst * tp), index // tp % hst, index % tp


def exchange(x, partner):
    _, hst, tp = sizes()
    pairs = []
    for index in range(sizes()[0] * hst * tp):
        o, h, t = partner(*coordinates(index))
        pairs.append((index, (o * hst + h) * tp + t))
    return lax.ppermute(x, AXES, pairs)


def pick(x, index):
    half = x.shape[0] // 2
    return jnp.where(index == 1, x[half:], x[:half])


def params(mib):
    return pltpu.CompilerParams(vmem_limit_bytes=mib * MIB)


def cost():
    return pl.CostEstimate(flops=10**6, bytes_accessed=0, transcendentals=0)


def whole():
    return pl.BlockSpec(memory_space=pltpu.VMEM)


def in_hbm(x):
    return pltpu.with_memory_space_constraint(x, pltpu.HBM)


def scalar():
    return pl.BlockSpec(memory_space=pltpu.SMEM)


def load(starts, rows, g_hbm, e_hbm, g_ref, e_ref, sems):
    chunks = []
    for c, start in enumerate(starts):
        source = pl.ds(pl.multiple_of(start, rows), rows)
        where = pl.ds(c * rows, rows)
        copies = [
            pltpu.make_async_copy(hbm.at[:, :, source, :], ref.at[:, :, where, :], sems.at[k, c])
            for k, (hbm, ref) in enumerate(((g_hbm, g_ref), (e_hbm, e_ref)))
        ]
        chunks.append((where, copies))
    return chunks


def start_all(copies):
    for copy in copies:
        copy.start(priority=1)


def wait_all(copies):
    for copy in copies:
        copy.wait()


FETCHES = 4


def mix_kernel(place_ref, q_hbm, g_hbm, e_hbm, *refs):
    first_ref, second_ref = refs[:2]
    mixed_ref = refs[2] if len(refs) == 9 else None
    q_ref, g_ref, e_ref, wide_ref, q_sem, sems = refs[-6:]
    m_count, pack, total_rows, width = g_ref.shape
    rank = q_ref.shape[1]
    count = place_ref.shape[0]
    rows = total_rows // count
    q_copy = pltpu.make_async_copy(q_hbm, q_ref, q_sem)
    q_copy.start()
    chunks = load([place_ref[c] * rows for c in range(count)], rows, g_hbm, e_hbm, g_ref, e_ref, sems)
    for _, copies in chunks[:FETCHES]:
        start_all(copies)
    lane_group = lax.broadcasted_iota(jnp.int32, (width, LANES), 1) // rank
    q_copy.wait()
    for m in range(m_count):
        turned = jnp.concatenate([q_ref[m]] * pack, axis=0).T
        for j in range(pack):
            wide_ref[m, pl.ds(j * width, width), :] = jnp.where(lane_group == j, turned, 0.0).astype(BF16)
    for c, (where, copies) in enumerate(chunks):
        wait_all(copies)
        if c + FETCHES < count:
            start_all(chunks[c + FETCHES][1])
        left_ref = first_ref if c < count // 2 else second_ref
        at = pl.ds(c % (count // 2) * rows, rows)
        for m in range(m_count):
            mixed = [g_ref[m, j, where, :] + e_ref[m, j, where, :] for j in range(pack)]
            total = jnp.dot(jnp.concatenate(mixed, axis=1), wide_ref[m], preferred_element_type=F32)
            left_ref[at, m * LANES:(m + 1) * LANES] = total.astype(left_ref.dtype)
            if mixed_ref is not None:
                for j in range(pack):
                    mixed_ref[m, j, where, :] = mixed[j]


def mix(gradient, error_acc, q_turned, first, second, rows, kept=False):
    m_count, pack, _, width = gradient.shape
    places = jnp.stack(first + second).astype(jnp.int32)
    count = len(first + second)
    shape = (m_count, pack, count * rows, width)
    hbm = pl.BlockSpec(memory_space=pltpu.HBM)
    return pl.pallas_call(
        mix_kernel,
        in_specs=[scalar()] + [hbm] * 3,
        out_specs=[whole()] * (2 + kept),
        out_shape=[pltpu.VMEM((len(first) * rows, m_count * LANES), dtype) for dtype in (BF16, F32)] + [pltpu.VMEM(shape, BF16)] * kept,
        scratch_shapes=[
            pltpu.VMEM(q_turned.shape, F32),
            pltpu.VMEM(shape, BF16),
            pltpu.VMEM(shape, BF16),
            pltpu.VMEM((m_count, pack * width, LANES), BF16),
            pltpu.SemaphoreType.DMA,
            pltpu.SemaphoreType.DMA((2, count)),
        ],
        compiler_params=params(20),
        cost_estimate=cost(),
        name="mix",
    )(places, q_turned, gradient, error_acc)


def keep_kernel(place_ref, g_hbm, e_hbm, mixed_ref, g_ref, e_ref, sems):
    count = place_ref.shape[0]
    rows = g_ref.shape[2] // count
    chunks = load([place_ref[c] * rows for c in range(count)], rows, g_hbm, e_hbm, g_ref, e_ref, sems)
    for _, copies in chunks:
        start_all(copies)
    for where, copies in chunks:
        wait_all(copies)
        mixed_ref[:, :, where, :] = g_ref[:, :, where, :] + e_ref[:, :, where, :]


def keep(gradient, error_acc, places, rows):
    m_count, pack, _, width = gradient.shape
    count = len(places)
    shape = (m_count, pack, count * rows, width)
    return pl.pallas_call(
        keep_kernel,
        in_specs=[scalar()] + [pl.BlockSpec(memory_space=pltpu.HBM)] * 2,
        out_specs=whole(),
        out_shape=pltpu.VMEM(shape, BF16),
        scratch_shapes=[pltpu.VMEM(shape, BF16), pltpu.VMEM(shape, BF16), pltpu.SemaphoreType.DMA((2, count))],
        compiler_params=params(16),
        cost_estimate=cost(),
        name="keep",
    )(jnp.stack(places).astype(jnp.int32), gradient, error_acc)


def project_kernel(chunks, *refs):
    count = len(chunks)
    lefts, right_ref, gram_ref = refs[:count], refs[-2], refs[-1]
    stores = 1 + max(store for store, _ in chunks)
    mixed = refs[count:count + stores]
    before = refs[count + stores:-2]
    m_count, pack, _, width = mixed[0].shape
    rank = LANES // pack
    right = [before[0][m] if before else jnp.zeros((rank, width), F32) for m in range(m_count)]
    for c, (store, place) in enumerate(chunks):
        left = lefts[c][...]
        rows = left.shape[0]
        turned = left.T
        every = jnp.dot(turned, left, preferred_element_type=F32)
        for m in range(m_count):
            gram = jnp.zeros((rank, rank), F32)
            for j in range(pack):
                at = m * LANES + j * rank
                gram += every[at:at + rank, at:at + rank]
                block = mixed[store][m, j, pl.ds(place * rows, rows), :]
                right[m] += jnp.dot(turned[at:at + rank], block, preferred_element_type=F32)
            gram_ref[c, m] = gram
    for m in range(m_count):
        right_ref[m] = right[m]


def project(lefts, mixed, chunks, *before):
    m_count, pack, _, width = mixed[0].shape
    rank = LANES // pack
    mixed = [pltpu.with_memory_space_constraint(x, pltpu.VMEM) for x in mixed]
    return pl.pallas_call(
        lambda *refs: project_kernel(chunks, *refs),
        in_specs=[whole()] * (len(lefts) + len(mixed) + len(before)),
        out_specs=[whole()] * 2,
        out_shape=[pltpu.VMEM((m_count, rank, width), F32), pltpu.VMEM((len(lefts), m_count, rank, rank), F32)],
        compiler_params=params(8),
        cost_estimate=cost(),
        name="project",
    )(*lefts, *mixed, *before)


def tree_sum(parts):
    while len(parts) > 1:
        parts = [parts[k] + parts[k + 1] for k in range(0, len(parts), 2)]
    return parts[0]


def invert_kernel(steps, *refs):
    grams, held_ref = refs[:-1], refs[-1]
    m_count, rank, _ = held_ref.shape
    row_at = lax.broadcasted_iota(jnp.int32, (rank, rank), 0)
    col_at = lax.broadcasted_iota(jnp.int32, (rank, rank), 1)
    held = [grams[0][m] for m in range(m_count)] if len(grams) == 1 else [
        tree_sum([grams[0][0, m]] + [grams[1][c, m] for c in range(grams[1].shape[0])])
        + tree_sum([grams[0][1, m]] + [grams[2][c, m] for c in range(grams[2].shape[0])])
        for m in range(m_count)
    ]
    for k in steps:
        for m in range(m_count):
            a = held[m]
            row, col = a[k:k + 1, :], a[:, k:k + 1]
            inv = 1.0 / a[k:k + 1, k:k + 1]
            scaled = row * inv
            rest = a - col * scaled
            rest = jnp.where(row_at == k, scaled, rest)
            held[m] = jnp.where(col_at == k, jnp.where(row_at == k, inv, -col * inv), rest)
    for m in range(m_count):
        held_ref[m] = held[m]


def invert(steps, *grams):
    return pl.pallas_call(
        lambda *refs: invert_kernel(steps, *refs),
        in_specs=[whole()] * len(grams),
        out_specs=whole(),
        out_shape=pltpu.VMEM(grams[0].shape[-3:], F32),
        compiler_params=params(4),
        cost_estimate=cost(),
        name="invert",
    )(*grams)


def three_parts(x):
    high = x.astype(BF16)
    rest = x - high.astype(F32)
    middle = rest.astype(BF16)
    return high, middle, (rest - middle.astype(F32)).astype(BF16)


def small_dot(a, b):
    a0, a1, a2 = three_parts(a)
    b0, b1, b2 = three_parts(b)
    wide = jnp.concatenate([a0, a0, a1, a1, a0, a2], axis=1)
    tall = jnp.concatenate([b0, b1, b0, b1, b2, b0], axis=0)
    return jnp.dot(wide, tall, preferred_element_type=F32)


def expand_kernel(scale, place_ref, left_ref, inverse_ref, right_ref, update_ref, wide_ref, held_ref, sems):
    m_count, rank, width = right_ref.shape
    pack = LANES // rank
    count, block, _ = left_ref.shape
    wide_ref[...] = jnp.zeros_like(wide_ref)
    copies = []
    for m in range(m_count):
        z = small_dot(inverse_ref[m], right_ref[m]) * scale
        high = z.astype(BF16)
        low = (z - high.astype(F32)).astype(BF16)
        for j in range(pack):
            wide_ref[m, j, pl.ds(j * rank, rank), :] = high
            wide_ref[m, j, pl.ds(LANES + j * rank, rank), :] = low
            for p in range(count):
                left = left_ref[p, :, m * LANES:(m + 1) * LANES]
                rows = jnp.dot(jnp.concatenate([left, left], axis=1), wide_ref[m, j], preferred_element_type=F32)
                held_ref[m, j, p] = rows.astype(BF16)
                where = pl.ds(pl.multiple_of(place_ref[p] * block, block), block)
                copy = pltpu.make_async_copy(held_ref.at[m, j, p], update_ref.at[m, j, where, :], sems.at[m, j, p])
                copy.start(priority=p % 2)
                copies.append(copy)
    for copy in copies:
        copy.wait()


def expand(pieces, places, inverse, right, scale):
    m_count, rank, width = right.shape
    pack = LANES // rank
    count, block, _ = pieces.shape
    out = pl.pallas_call(
        lambda *refs: expand_kernel(scale, *refs),
        in_specs=[scalar(), whole(), whole(), whole()],
        out_specs=pl.BlockSpec(memory_space=pl.ANY),
        out_shape=jax.ShapeDtypeStruct((m_count, pack, count * block, width), BF16),
        scratch_shapes=[
            pltpu.VMEM((m_count, pack, 2 * LANES, width), BF16),
            pltpu.VMEM((m_count, pack, count, block, width), BF16),
            pltpu.SemaphoreType.DMA((m_count, pack, count)),
        ],
        compiler_params=params(20),
        name="expand",
    )(places, pieces, inverse, right)
    return out.reshape(m_count, pack * count * block, width)


def sum_right(right, grams):
    outer, hst, _ = sizes()
    rank = right.shape[1]
    for b in range(bits(hst)):
        right = right + exchange(right, lambda o, h, t, b=b: (o, h ^ (1 << b), t))
    early = rank // 4
    right, inverse = after(right, invert(range(early), *grams))
    parts = [right] + [exchange(right, lambda o, h, t, k=k: (o ^ k, h, t)) for k in range(1, outer)]
    inverse = invert(range(early, rank), inverse)
    return tree_sum(parts), inverse


def after(value, *others):
    return lax.optimization_barrier((value, *others))


def shards(gradient, error_acc, q_start):
    _, m_count, depth, width = gradient.shape
    outer, hst, tp = sizes()
    rows = depth // PACK
    chunk = rows // (2 * outer)
    shape = (m_count, PACK, rows, width)
    gradient, error_acc = in_hbm(gradient.reshape(shape)), in_hbm(error_acc.reshape(shape))
    q_turned = in_hbm(jnp.swapaxes(q_start, 1, 2))
    o, h = lax.axis_index("outer"), lax.axis_index("hst")
    near = [(h & 1) * outer + (o ^ k) for k in range(outer)]
    far = [(1 - (h & 1)) * outer + (o ^ k) for k in range(outer)]

    def core(x):
        return exchange(x, lambda o, h, t: (o, h ^ 1, t))

    def chip(x, k):
        return exchange(x, lambda o, h, t: (o ^ k, h, t))

    def after_all(value, places):
        value, *places = after(value, *places)
        return value, places

    left_far, left = mix(gradient, error_acc, q_turned, far[1:], near[1:], chunk)
    sent = (left + core(left_far).astype(F32)).astype(BF16)
    sent, (at_far, at_near) = after_all(sent, [far[0], near[0]])
    came = [chip(sent[(k - 1) * chunk:k * chunk], k) for k in range(1, outer)]
    left_far, left, mixed_own = mix(gradient, error_acc, q_turned, [at_far], [at_near], chunk, True)
    left = left + core(left_far).astype(F32)
    for part in came:
        left = left + part.astype(F32)
    for b in range(1, bits(hst)):
        bit = (h >> b) & 1
        sent = pick(left, 1 - bit).astype(BF16)
        left = pick(left, bit) + exchange(sent, lambda o, h, t, b=b: (o, h ^ (1 << b), t)).astype(F32)
    others = near[1:] + far[1:]
    early, late = len(others) // 3, len(others) // 2
    waiting, mixed = [others[:early], others[early:late]], []
    for b in range(bits(tp)):
        sent = left.astype(BF16)
        places = waiting.pop(0) if waiting else None
        if places:
            sent, places = after_all(sent, places)
            kept = keep(gradient, error_acc, places, chunk)
        got = exchange(sent, lambda o, h, t, b=b: (o, h, t ^ (1 << (b if h % 2 == 0 else bits(tp) - 1 - b))))
        if places:
            got, kept = after(got, kept)
            mixed.append(kept)
        left = sent.astype(F32) + got.astype(F32)
    mixed += [keep(gradient, error_acc, places, chunk) for places in waiting]
    own = left.astype(BF16)

    for b in reversed(range(1, bits(hst))):
        bit = (h >> b) & 1
        got = exchange(own, lambda o, h, t, b=b: (o, h ^ (1 << b), t))
        own = jnp.concatenate([jnp.where(bit == 1, got, own), jnp.where(bit == 1, own, got)])
    own, places = after_all(own, others[late:])
    near_left, far_left = [own], [core(own)]
    came = [chip(own, k) for k in range(1, outer)]
    right, gram_own = project([own, far_left[0]], [mixed_own], [(0, 1), (0, 0)])
    mixed.append(keep(gradient, error_acc, places, chunk))
    came[-1], right, mixed[2] = after(came[-1], right, mixed[2])
    near_left += came
    far_left += [core(part) for part in came]
    where = [(0, k) for k in range(early)] + [(1, k) for k in range(late - early)] + [(2, k) for k in range(len(others) - late)]
    n = outer - 1

    def project_others(lefts, chunks, right):
        used = sorted({store for store, _ in chunks})
        chunks = [(used.index(store), place) for store, place in chunks]
        return project(lefts, [mixed[store] for store in used], chunks, right)

    right, gram_near = project_others(near_left[1:], where[:n], right)
    right, gram_far = project_others(far_left[1:], where[n:], right)

    right, inverse = sum_right(right, (gram_own, gram_near, gram_far))
    pieces = jnp.stack(near_left + far_left)
    places = jnp.stack(near + far).astype(jnp.int32)
    return expand(pieces, places, inverse, right, 1.0 / (outer * hst))


def solution(mesh):
    in_specs = (
        P(("outer", "hst"), None, None, "tp"),
        P(("outer", "hst"), None, None, "tp"),
        P(None, "tp", None),
    )
    out_specs = P(None, None, "tp")
    return jax.shard_map(shards, mesh=mesh, in_specs=in_specs, out_specs=out_specs, check_vma=False)
```

```python
import jax
import jax.numpy as jnp
from jax import lax
from jax.experimental import pallas as pl
from jax.experimental.pallas import tpu as pltpu
from jax.sharding import PartitionSpec as P

AXES = ("outer", "hst", "tp")
PACK = 4
LANES = 128
F32, BF16 = jnp.float32, jnp.bfloat16
MIB = 1024 * 1024


def bits(size):
    return size.bit_length() - 1


def sizes():
    return tuple(lax.axis_size(axis) for axis in AXES)


def coordinates(index):
    _, hst, tp = sizes()
    return index // (hst * tp), index // tp % hst, index % tp


def exchange(x, partner):
    _, hst, tp = sizes()
    pairs = []
    for index in range(sizes()[0] * hst * tp):
        o, h, t = partner(*coordinates(index))
        pairs.append((index, (o * hst + h) * tp + t))
    return lax.ppermute(x, AXES, pairs)


def pick(x, index):
    half = x.shape[0] // 2
    return jnp.where(index == 1, x[half:], x[:half])


def params(mib):
    return pltpu.CompilerParams(vmem_limit_bytes=mib * MIB)


def cost():
    return pl.CostEstimate(flops=10**6, bytes_accessed=0, transcendentals=0)


def whole():
    return pl.BlockSpec(memory_space=pltpu.VMEM)


def in_hbm(x):
    return pltpu.with_memory_space_constraint(x, pltpu.HBM)


def scalar():
    return pl.BlockSpec(memory_space=pltpu.SMEM)


def load(starts, rows, g_hbm, e_hbm, g_ref, e_ref, sems):
    chunks = []
    for c, start in enumerate(starts):
        source = pl.ds(pl.multiple_of(start, rows), rows)
        where = pl.ds(c * rows, rows)
        copies = [
            pltpu.make_async_copy(hbm.at[:, :, source, :], ref.at[:, :, where, :], sems.at[k, c])
            for k, (hbm, ref) in enumerate(((g_hbm, g_ref), (e_hbm, e_ref)))
        ]
        chunks.append((where, copies))
    return chunks


def start_all(copies):
    for copy in copies:
        copy.start(priority=1)


def wait_all(copies):
    for copy in copies:
        copy.wait()


FETCHES = 4


def mix_kernel(place_ref, q_hbm, g_hbm, e_hbm, *refs):
    first_ref, second_ref = refs[:2]
    mixed_ref = refs[2] if len(refs) == 9 else None
    q_ref, g_ref, e_ref, wide_ref, q_sem, sems = refs[-6:]
    m_count, pack, total_rows, width = g_ref.shape
    rank = q_ref.shape[1]
    count = place_ref.shape[0]
    rows = total_rows // count
    q_copy = pltpu.make_async_copy(q_hbm, q_ref, q_sem)
    q_copy.start()
    chunks = load([place_ref[c] * rows for c in range(count)], rows, g_hbm, e_hbm, g_ref, e_ref, sems)
    for _, copies in chunks[:FETCHES]:
        start_all(copies)
    lane_group = lax.broadcasted_iota(jnp.int32, (width, LANES), 1) // rank
    q_copy.wait()
    for m in range(m_count):
        turned = jnp.concatenate([q_ref[m]] * pack, axis=0).T
        for j in range(pack):
            wide_ref[m, pl.ds(j * width, width), :] = jnp.where(lane_group == j, turned, 0.0).astype(BF16)
    for c, (where, copies) in enumerate(chunks):
        wait_all(copies)
        if c + FETCHES < count:
            start_all(chunks[c + FETCHES][1])
        left_ref = first_ref if c < count // 2 else second_ref
        at = pl.ds(c % (count // 2) * rows, rows)
        for m in range(m_count):
            mixed = [g_ref[m, j, where, :] + e_ref[m, j, where, :] for j in range(pack)]
            total = jnp.dot(jnp.concatenate(mixed, axis=1), wide_ref[m], preferred_element_type=F32)
            left_ref[at, m * LANES:(m + 1) * LANES] = total.astype(left_ref.dtype)
            if mixed_ref is not None:
                for j in range(pack):
                    mixed_ref[m, j, where, :] = mixed[j]


def mix(gradient, error_acc, q_turned, first, second, rows, kept=False):
    m_count, pack, _, width = gradient.shape
    places = jnp.stack(first + second).astype(jnp.int32)
    count = len(first + second)
    shape = (m_count, pack, count * rows, width)
    hbm = pl.BlockSpec(memory_space=pltpu.HBM)
    return pl.pallas_call(
        mix_kernel,
        in_specs=[scalar()] + [hbm] * 3,
        out_specs=[whole()] * (2 + kept),
        out_shape=[pltpu.VMEM((len(first) * rows, m_count * LANES), dtype) for dtype in (BF16, F32)] + [pltpu.VMEM(shape, BF16)] * kept,
        scratch_shapes=[
            pltpu.VMEM(q_turned.shape, F32),
            pltpu.VMEM(shape, BF16),
            pltpu.VMEM(shape, BF16),
            pltpu.VMEM((m_count, pack * width, LANES), BF16),
            pltpu.SemaphoreType.DMA,
            pltpu.SemaphoreType.DMA((2, count)),
        ],
        compiler_params=params(20),
        cost_estimate=cost(),
        name="mix",
    )(places, q_turned, gradient, error_acc)


def keep_kernel(place_ref, g_hbm, e_hbm, mixed_ref, g_ref, e_ref, sems):
    count = place_ref.shape[0]
    rows = g_ref.shape[2] // count
    chunks = load([place_ref[c] * rows for c in range(count)], rows, g_hbm, e_hbm, g_ref, e_ref, sems)
    for _, copies in chunks:
        start_all(copies)
    for where, copies in chunks:
        wait_all(copies)
        mixed_ref[:, :, where, :] = g_ref[:, :, where, :] + e_ref[:, :, where, :]


def keep(gradient, error_acc, places, rows):
    m_count, pack, _, width = gradient.shape
    count = len(places)
    shape = (m_count, pack, count * rows, width)
    return pl.pallas_call(
        keep_kernel,
        in_specs=[scalar()] + [pl.BlockSpec(memory_space=pltpu.HBM)] * 2,
        out_specs=whole(),
        out_shape=pltpu.VMEM(shape, BF16),
        scratch_shapes=[pltpu.VMEM(shape, BF16), pltpu.VMEM(shape, BF16), pltpu.SemaphoreType.DMA((2, count))],
        compiler_params=params(16),
        cost_estimate=cost(),
        name="keep",
    )(jnp.stack(places).astype(jnp.int32), gradient, error_acc)


def project_kernel(chunks, *refs):
    count = len(chunks)
    lefts, right_ref, gram_ref = refs[:count], refs[-2], refs[-1]
    stores = 1 + max(store for store, _ in chunks)
    mixed = refs[count:count + stores]
    before = refs[count + stores:-2]
    m_count, pack, _, width = mixed[0].shape
    rank = LANES // pack
    right = [before[0][m] if before else jnp.zeros((rank, width), F32) for m in range(m_count)]
    for c, (store, place) in enumerate(chunks):
        left = lefts[c][...]
        rows = left.shape[0]
        turned = left.T
        every = jnp.dot(turned, left, preferred_element_type=F32)
        for m in range(m_count):
            gram = jnp.zeros((rank, rank), F32)
            for j in range(pack):
                at = m * LANES + j * rank
                gram += every[at:at + rank, at:at + rank]
                block = mixed[store][m, j, pl.ds(place * rows, rows), :]
                right[m] += jnp.dot(turned[at:at + rank], block, preferred_element_type=F32)
            gram_ref[c, m] = gram
    for m in range(m_count):
        right_ref[m] = right[m]


def project(lefts, mixed, chunks, *before):
    m_count, pack, _, width = mixed[0].shape
    rank = LANES // pack
    mixed = [pltpu.with_memory_space_constraint(x, pltpu.VMEM) for x in mixed]
    return pl.pallas_call(
        lambda *refs: project_kernel(chunks, *refs),
        in_specs=[whole()] * (len(lefts) + len(mixed) + len(before)),
        out_specs=[whole()] * 2,
        out_shape=[pltpu.VMEM((m_count, rank, width), F32), pltpu.VMEM((len(lefts), m_count, rank, rank), F32)],
        compiler_params=params(8),
        cost_estimate=cost(),
        name="project",
    )(*lefts, *mixed, *before)


def tree_sum(parts):
    while len(parts) > 1:
        parts = [parts[k] + parts[k + 1] for k in range(0, len(parts), 2)]
    return parts[0]


def invert_kernel(steps, *refs):
    grams, held_ref = refs[:-1], refs[-1]
    m_count, rank, _ = held_ref.shape
    row_at = lax.broadcasted_iota(jnp.int32, (rank, rank), 0)
    col_at = lax.broadcasted_iota(jnp.int32, (rank, rank), 1)
    lane = lax.broadcasted_iota(jnp.int32, (1, rank), 1)
    held = [grams[0][m] for m in range(m_count)] if len(grams) == 1 else [
        tree_sum([grams[0][0, m]] + [grams[1][c, m] for c in range(grams[1].shape[0])])
        + tree_sum([grams[0][1, m]] + [grams[2][c, m] for c in range(grams[2].shape[0])])
        for m in range(m_count)
    ]
    for k in steps:
        for m in range(m_count):
            a = held[m]
            row, col = a[k:k + 1, :], a[:, k:k + 1]
            scaled = jnp.where(lane == k, 1.0, row) * (1.0 / a[k:k + 1, k:k + 1])
            held[m] = jnp.where(row_at == k, scaled, jnp.where(col_at == k, 0.0, a) - col * scaled)
    for m in range(m_count):
        held_ref[m] = held[m]


def invert(steps, *grams):
    return pl.pallas_call(
        lambda *refs: invert_kernel(steps, *refs),
        in_specs=[whole()] * len(grams),
        out_specs=whole(),
        out_shape=pltpu.VMEM(grams[0].shape[-3:], F32),
        compiler_params=params(4),
        cost_estimate=cost(),
        name="invert",
    )(*grams)


def three_parts(x):
    high = x.astype(BF16)
    rest = x - high.astype(F32)
    middle = rest.astype(BF16)
    return high, middle, (rest - middle.astype(F32)).astype(BF16)


def small_dot(a, b):
    a0, a1, a2 = three_parts(a)
    b0, b1, b2 = three_parts(b)
    wide = jnp.concatenate([a0, a0, a1, a1, a0, a2], axis=1)
    tall = jnp.concatenate([b0, b1, b0, b1, b2, b0], axis=0)
    return jnp.dot(wide, tall, preferred_element_type=F32)


EXPAND_ROWS = 512


def expand_kernel(scale, left_ref, inverse_ref, right_ref, update_ref, wide_ref, held_ref, sems):
    m_count, rank, width = right_ref.shape
    pack = LANES // rank
    copies = []
    for m in range(m_count):
        z = small_dot(inverse_ref[m], right_ref[m]) * scale
        high = z.astype(BF16)
        low = (z - high.astype(F32)).astype(BF16)
        wide_ref[m] = jnp.zeros(wide_ref.shape[1:], BF16)
        for j in range(pack):
            wide_ref[m, j, pl.ds(j * rank, rank), :] = high
            wide_ref[m, j, pl.ds(LANES + j * rank, rank), :] = low
            for p in range(left_ref.shape[0] // EXPAND_ROWS):
                where = pl.ds(p * EXPAND_ROWS, EXPAND_ROWS)
                left = left_ref[where, m * LANES:(m + 1) * LANES]
                rows = jnp.dot(jnp.concatenate([left, left], axis=1), wide_ref[m, j], preferred_element_type=F32)
                held_ref[m, j, where, :] = rows.astype(BF16)
                copy = pltpu.make_async_copy(held_ref.at[m, j, where, :], update_ref.at[m, j, where, :], sems.at[m, j, p])
                copy.start(priority=p % 2)
                copies.append(copy)
    wait_all(copies)


def expand(left, inverse, right, scale):
    m_count, rank, width = right.shape
    pack = LANES // rank
    rows = left.shape[0]
    shape = (m_count, pack, rows, width)
    out = pl.pallas_call(
        lambda *refs: expand_kernel(scale, *refs),
        in_specs=[whole()] * 3,
        out_specs=pl.BlockSpec(memory_space=pl.ANY),
        out_shape=jax.ShapeDtypeStruct(shape, BF16),
        scratch_shapes=[
            pltpu.VMEM((m_count, pack, 2 * LANES, width), BF16),
            pltpu.VMEM(shape, BF16),
            pltpu.SemaphoreType.DMA((m_count, pack, rows // EXPAND_ROWS)),
        ],
        compiler_params=params(20),
        name="expand",
    )(left, inverse, right)
    return out.reshape(m_count, pack * rows, width)


def sum_right(right, grams):
    outer, hst, _ = sizes()
    rank = right.shape[1]
    for b in range(bits(hst)):
        right = right + exchange(right, lambda o, h, t, b=b: (o, h ^ (1 << b), t))
    early = rank // 4
    right, inverse = after(right, invert(range(early), *grams))
    parts = [right] + [exchange(right, lambda o, h, t, k=k: (o ^ k, h, t)) for k in range(1, outer)]
    inverse = invert(range(early, rank), inverse)
    return tree_sum(parts), inverse


def after(value, *others):
    return lax.optimization_barrier((value, *others))


def shards(gradient, error_acc, q_start):
    _, m_count, depth, width = gradient.shape
    outer, hst, tp = sizes()
    rows = depth // PACK
    chunk = rows // (2 * outer)
    shape = (m_count, PACK, rows, width)
    gradient, error_acc = in_hbm(gradient.reshape(shape)), in_hbm(error_acc.reshape(shape))
    q_turned = in_hbm(jnp.swapaxes(q_start, 1, 2))
    o, h = lax.axis_index("outer"), lax.axis_index("hst")
    near = [(h & 1) * outer + (o ^ k) for k in range(outer)]
    far = [(1 - (h & 1)) * outer + (o ^ k) for k in range(outer)]

    def core(x):
        return exchange(x, lambda o, h, t: (o, h ^ 1, t))

    def chip(x, k):
        return exchange(x, lambda o, h, t: (o ^ k, h, t))

    def after_all(value, places):
        value, *places = after(value, *places)
        return value, places

    left_far, left = mix(gradient, error_acc, q_turned, far[1:], near[1:], chunk)
    sent = (left + core(left_far).astype(F32)).astype(BF16)
    sent, (at_far, at_near) = after_all(sent, [far[0], near[0]])
    came = [chip(sent[(k - 1) * chunk:k * chunk], k) for k in range(1, outer)]
    left_far, left, mixed_own = mix(gradient, error_acc, q_turned, [at_far], [at_near], chunk, True)
    left = left + core(left_far).astype(F32)
    for part in came:
        left = left + part.astype(F32)
    for b in range(1, bits(hst)):
        bit = (h >> b) & 1
        sent = pick(left, 1 - bit).astype(BF16)
        left = pick(left, bit) + exchange(sent, lambda o, h, t, b=b: (o, h ^ (1 << b), t)).astype(F32)
    others = near[1:] + far[1:]
    early, late = len(others) // 3, len(others) // 2
    waiting, mixed = [others[:early], others[early:late]], []
    for b in range(bits(tp)):
        sent = left.astype(BF16)
        places = waiting.pop(0) if waiting else None
        if places:
            sent, places = after_all(sent, places)
            kept = keep(gradient, error_acc, places, chunk)
        got = exchange(sent, lambda o, h, t, b=b: (o, h, t ^ (1 << (b if h % 2 == 0 else bits(tp) - 1 - b))))
        if places:
            got, kept = after(got, kept)
            mixed.append(kept)
        left = sent.astype(F32) + got.astype(F32)
    mixed += [keep(gradient, error_acc, places, chunk) for places in waiting]
    own = left.astype(BF16)

    for b in reversed(range(1, bits(hst))):
        bit = (h >> b) & 1
        got = exchange(own, lambda o, h, t, b=b: (o, h ^ (1 << b), t))
        own = jnp.concatenate([jnp.where(bit == 1, got, own), jnp.where(bit == 1, own, got)])
    own, places = after_all(own, others[late:])
    near_left, far_left = [own], [core(own)]
    came = [chip(own, k) for k in range(1, outer)]
    right, gram_own = project([own, far_left[0]], [mixed_own], [(0, 1), (0, 0)])
    mixed.append(keep(gradient, error_acc, places, chunk))
    came[-1], right, mixed[2] = after(came[-1], right, mixed[2])
    near_left += came
    far_left += [core(part) for part in came]
    where = [(0, k) for k in range(early)] + [(1, k) for k in range(late - early)] + [(2, k) for k in range(len(others) - late)]
    n = outer - 1

    def project_others(lefts, chunks, right):
        used = sorted({store for store, _ in chunks})
        chunks = [(used.index(store), place) for store, place in chunks]
        return project(lefts, [mixed[store] for store in used], chunks, right)

    right, gram_near = project_others(near_left[1:], where[:n], right)
    right, gram_far = project_others(far_left[1:], where[n:], right)

    right, inverse = sum_right(right, (gram_own, gram_near, gram_far))
    left = jnp.zeros((rows, own.shape[1]), BF16)
    for place, part in zip(near + far, near_left + far_left):
        left = lax.dynamic_update_slice(left, part, (place * chunk, 0))
    return expand(left, inverse, right, 1.0 / (outer * hst))


def solution(mesh):
    in_specs = (
        P(("outer", "hst"), None, None, "tp"),
        P(("outer", "hst"), None, None, "tp"),
        P(None, "tp", None),
    )
    out_specs = P(None, None, "tp")
    return jax.shard_map(shards, mesh=mesh, in_specs=in_specs, out_specs=out_specs, check_vma=False)
```

```python
import jax
import jax.numpy as jnp
from jax import lax
from jax.experimental import pallas as pl
from jax.experimental.pallas import tpu as pltpu
from jax.sharding import PartitionSpec as P

AXES = ("outer", "hst", "tp")
PACK = 4
LANES = 128
F32, BF16 = jnp.float32, jnp.bfloat16
MIB = 1024 * 1024


def bits(size):
    return size.bit_length() - 1


def sizes():
    return tuple(lax.axis_size(axis) for axis in AXES)


def coordinates(index):
    _, hst, tp = sizes()
    return index // (hst * tp), index // tp % hst, index % tp


def exchange(x, partner):
    _, hst, tp = sizes()
    pairs = []
    for index in range(sizes()[0] * hst * tp):
        o, h, t = partner(*coordinates(index))
        pairs.append((index, (o * hst + h) * tp + t))
    return lax.ppermute(x, AXES, pairs)


def pick(x, index):
    half = x.shape[0] // 2
    return jnp.where(index == 1, x[half:], x[:half])


def params(mib):
    return pltpu.CompilerParams(vmem_limit_bytes=mib * MIB)


def cost():
    return pl.CostEstimate(flops=10**6, bytes_accessed=0, transcendentals=0)


def whole():
    return pl.BlockSpec(memory_space=pltpu.VMEM)


def in_hbm(x):
    return pltpu.with_memory_space_constraint(x, pltpu.HBM)


def scalar():
    return pl.BlockSpec(memory_space=pltpu.SMEM)


def load(starts, rows, g_hbm, e_hbm, g_ref, e_ref, sems):
    chunks = []
    for c, start in enumerate(starts):
        source = pl.ds(pl.multiple_of(start, rows), rows)
        where = pl.ds(c * rows, rows)
        copies = [
            pltpu.make_async_copy(hbm.at[:, :, source, :], ref.at[:, :, where, :], sems.at[k, c])
            for k, (hbm, ref) in enumerate(((g_hbm, g_ref), (e_hbm, e_ref)))
        ]
        chunks.append((where, copies))
    return chunks


def start_all(copies):
    for copy in copies:
        copy.start(priority=1)


def wait_all(copies):
    for copy in copies:
        copy.wait()


FETCHES = 4


def mix_kernel(place_ref, q_hbm, g_hbm, e_hbm, *refs):
    first_ref, second_ref = refs[:2]
    mixed_ref = refs[2] if len(refs) == 9 else None
    q_ref, g_ref, e_ref, wide_ref, q_sem, sems = refs[-6:]
    m_count, pack, total_rows, width = g_ref.shape
    rank = q_ref.shape[1]
    count = place_ref.shape[0]
    rows = total_rows // count
    q_copy = pltpu.make_async_copy(q_hbm, q_ref, q_sem)
    q_copy.start()
    chunks = load([place_ref[c] * rows for c in range(count)], rows, g_hbm, e_hbm, g_ref, e_ref, sems)
    for _, copies in chunks[:FETCHES]:
        start_all(copies)
    lane_group = lax.broadcasted_iota(jnp.int32, (width, LANES), 1) // rank
    q_copy.wait()
    for m in range(m_count):
        turned = jnp.concatenate([q_ref[m]] * pack, axis=0).T
        for j in range(pack):
            wide_ref[m, pl.ds(j * width, width), :] = jnp.where(lane_group == j, turned, 0.0).astype(BF16)
    for c, (where, copies) in enumerate(chunks):
        wait_all(copies)
        if c + FETCHES < count:
            start_all(chunks[c + FETCHES][1])
        left_ref = first_ref if c < count // 2 else second_ref
        at = pl.ds(c % (count // 2) * rows, rows)
        for m in range(m_count):
            mixed = [g_ref[m, j, where, :] + e_ref[m, j, where, :] for j in range(pack)]
            total = jnp.dot(jnp.concatenate(mixed, axis=1), wide_ref[m], preferred_element_type=F32)
            left_ref[at, m * LANES:(m + 1) * LANES] = total.astype(left_ref.dtype)
            if mixed_ref is not None:
                for j in range(pack):
                    mixed_ref[m, j, where, :] = mixed[j]


def mix(gradient, error_acc, q_turned, first, second, rows, kept=False):
    m_count, pack, _, width = gradient.shape
    places = jnp.stack(first + second).astype(jnp.int32)
    count = len(first + second)
    shape = (m_count, pack, count * rows, width)
    hbm = pl.BlockSpec(memory_space=pltpu.HBM)
    return pl.pallas_call(
        mix_kernel,
        in_specs=[scalar()] + [hbm] * 3,
        out_specs=[whole()] * (2 + kept),
        out_shape=[pltpu.VMEM((len(first) * rows, m_count * LANES), dtype) for dtype in (BF16, F32)] + [pltpu.VMEM(shape, BF16)] * kept,
        scratch_shapes=[
            pltpu.VMEM(q_turned.shape, F32),
            pltpu.VMEM(shape, BF16),
            pltpu.VMEM(shape, BF16),
            pltpu.VMEM((m_count, pack * width, LANES), BF16),
            pltpu.SemaphoreType.DMA,
            pltpu.SemaphoreType.DMA((2, count)),
        ],
        compiler_params=params(20),
        cost_estimate=cost(),
        name="mix",
    )(places, q_turned, gradient, error_acc)


def keep_kernel(place_ref, g_hbm, e_hbm, mixed_ref, g_ref, e_ref, sems):
    count = place_ref.shape[0]
    rows = g_ref.shape[2] // count
    chunks = load([place_ref[c] * rows for c in range(count)], rows, g_hbm, e_hbm, g_ref, e_ref, sems)
    for _, copies in chunks:
        start_all(copies)
    for where, copies in chunks:
        wait_all(copies)
        mixed_ref[:, :, where, :] = g_ref[:, :, where, :] + e_ref[:, :, where, :]


def keep(gradient, error_acc, places, rows):
    m_count, pack, _, width = gradient.shape
    count = len(places)
    shape = (m_count, pack, count * rows, width)
    return pl.pallas_call(
        keep_kernel,
        in_specs=[scalar()] + [pl.BlockSpec(memory_space=pltpu.HBM)] * 2,
        out_specs=whole(),
        out_shape=pltpu.VMEM(shape, BF16),
        scratch_shapes=[pltpu.VMEM(shape, BF16), pltpu.VMEM(shape, BF16), pltpu.SemaphoreType.DMA((2, count))],
        compiler_params=params(16),
        cost_estimate=cost(),
        name="keep",
    )(jnp.stack(places).astype(jnp.int32), gradient, error_acc)


def project_kernel(chunks, *refs):
    count = len(chunks)
    lefts, right_ref, gram_ref = refs[:count], refs[-2], refs[-1]
    stores = 1 + max(store for store, _ in chunks)
    mixed = refs[count:count + stores]
    before = refs[count + stores:-2]
    m_count, pack, _, width = mixed[0].shape
    rank = LANES // pack
    right = [before[0][m] if before else jnp.zeros((rank, width), F32) for m in range(m_count)]
    for c, (store, place) in enumerate(chunks):
        left = lefts[c][...]
        rows = left.shape[0]
        turned = left.T
        every = jnp.dot(turned, left, preferred_element_type=F32)
        for m in range(m_count):
            gram = jnp.zeros((rank, rank), F32)
            for j in range(pack):
                at = m * LANES + j * rank
                gram += every[at:at + rank, at:at + rank]
                block = mixed[store][m, j, pl.ds(place * rows, rows), :]
                right[m] += jnp.dot(turned[at:at + rank], block, preferred_element_type=F32)
            gram_ref[c, m] = gram
    for m in range(m_count):
        right_ref[m] = right[m]


def project(lefts, mixed, chunks, *before):
    m_count, pack, _, width = mixed[0].shape
    rank = LANES // pack
    mixed = [pltpu.with_memory_space_constraint(x, pltpu.VMEM) for x in mixed]
    return pl.pallas_call(
        lambda *refs: project_kernel(chunks, *refs),
        in_specs=[whole()] * (len(lefts) + len(mixed) + len(before)),
        out_specs=[whole()] * 2,
        out_shape=[pltpu.VMEM((m_count, rank, width), F32), pltpu.VMEM((len(lefts), m_count, rank, rank), F32)],
        compiler_params=params(8),
        cost_estimate=cost(),
        name="project",
    )(*lefts, *mixed, *before)


def tree_sum(parts):
    while len(parts) > 1:
        parts = [parts[k] + parts[k + 1] for k in range(0, len(parts), 2)]
    return parts[0]


def invert_kernel(steps, *refs):
    grams, held_ref = refs[:-1], refs[-1]
    m_count, rank, _ = held_ref.shape
    row_at = lax.broadcasted_iota(jnp.int32, (rank, rank), 0)
    col_at = lax.broadcasted_iota(jnp.int32, (rank, rank), 1)
    lane = lax.broadcasted_iota(jnp.int32, (1, rank), 1)
    held = [grams[0][m] for m in range(m_count)] if len(grams) == 1 else [
        tree_sum([grams[0][0, m]] + [grams[1][c, m] for c in range(grams[1].shape[0])])
        + tree_sum([grams[0][1, m]] + [grams[2][c, m] for c in range(grams[2].shape[0])])
        for m in range(m_count)
    ]
    for k in steps:
        for m in range(m_count):
            a = held[m]
            row, col = a[k:k + 1, :], a[:, k:k + 1]
            scaled = jnp.where(lane == k, 1.0, row) * (1.0 / a[k:k + 1, k:k + 1])
            held[m] = jnp.where(row_at == k, scaled, jnp.where(col_at == k, 0.0, a) - col * scaled)
    for m in range(m_count):
        held_ref[m] = held[m]


def invert(steps, *grams):
    return pl.pallas_call(
        lambda *refs: invert_kernel(steps, *refs),
        in_specs=[whole()] * len(grams),
        out_specs=whole(),
        out_shape=pltpu.VMEM(grams[0].shape[-3:], F32),
        compiler_params=params(4),
        cost_estimate=cost(),
        name="invert",
    )(*grams)


def three_parts(x):
    high = x.astype(BF16)
    rest = x - high.astype(F32)
    middle = rest.astype(BF16)
    return high, middle, (rest - middle.astype(F32)).astype(BF16)


def small_dot(a, b):
    a0, a1, a2 = three_parts(a)
    b0, b1, b2 = three_parts(b)
    wide = jnp.concatenate([a0, a0, a1, a1, a0, a2], axis=1)
    tall = jnp.concatenate([b0, b1, b0, b1, b2, b0], axis=0)
    return jnp.dot(wide, tall, preferred_element_type=F32)


EXPAND_ROWS = 512


def expand_kernel(scale, left_ref, inverse_ref, right_ref, update_ref, wide_ref, held_ref, sems):
    m_count, rank, width = right_ref.shape
    pack = LANES // rank
    copies = []
    for m in range(m_count):
        z = small_dot(inverse_ref[m], right_ref[m]) * scale
        high = z.astype(BF16)
        low = (z - high.astype(F32)).astype(BF16)
        wide_ref[m] = jnp.zeros(wide_ref.shape[1:], BF16)
        for j in range(pack):
            wide_ref[m, j, pl.ds(j * rank, rank), :] = high
            wide_ref[m, j, pl.ds(LANES + j * rank, rank), :] = low
            for p in range(left_ref.shape[0] // EXPAND_ROWS):
                where = pl.ds(p * EXPAND_ROWS, EXPAND_ROWS)
                left = left_ref[where, m * LANES:(m + 1) * LANES]
                rows = jnp.dot(jnp.concatenate([left, left], axis=1), wide_ref[m, j], preferred_element_type=F32)
                held_ref[m, j, where, :] = rows.astype(BF16)
                copy = pltpu.make_async_copy(held_ref.at[m, j, where, :], update_ref.at[m, j, where, :], sems.at[m, j, p])
                copy.start(priority=p % 2)
                copies.append(copy)
    wait_all(copies)


def expand(left, inverse, right, scale):
    m_count, rank, width = right.shape
    pack = LANES // rank
    rows = left.shape[0]
    shape = (m_count, pack, rows, width)
    out = pl.pallas_call(
        lambda *refs: expand_kernel(scale, *refs),
        in_specs=[whole()] * 3,
        out_specs=pl.BlockSpec(memory_space=pl.ANY),
        out_shape=jax.ShapeDtypeStruct(shape, BF16),
        scratch_shapes=[
            pltpu.VMEM((m_count, pack, 2 * LANES, width), BF16),
            pltpu.VMEM(shape, BF16),
            pltpu.SemaphoreType.DMA((m_count, pack, rows // EXPAND_ROWS)),
        ],
        compiler_params=params(20),
        name="expand",
    )(left, inverse, right)
    return out.reshape(m_count, pack * rows, width)


def sum_right(right, grams):
    outer, hst, _ = sizes()
    rank = right.shape[1]
    for b in range(bits(hst)):
        right = right + exchange(right, lambda o, h, t, b=b: (o, h ^ (1 << b), t))
    early = rank // 4
    right, inverse = after(right, invert(range(early), *grams))
    right = right.astype(BF16)
    parts = [right] + [exchange(right, lambda o, h, t, k=k: (o ^ k, h, t)) for k in range(1, outer)]
    inverse = invert(range(early, rank), inverse)
    return tree_sum([part.astype(F32) for part in parts]), inverse


def turned(k):
    n = bits(lax.axis_size("outer"))
    return sum(((k >> b) & 1) << (n - 1 - b) for b in range(n))


def after(value, *others):
    return lax.optimization_barrier((value, *others))


def shards(gradient, error_acc, q_start):
    _, m_count, depth, width = gradient.shape
    outer, hst, tp = sizes()
    rows = depth // PACK
    chunk = rows // (2 * outer)
    shape = (m_count, PACK, rows, width)
    gradient, error_acc = in_hbm(gradient.reshape(shape)), in_hbm(error_acc.reshape(shape))
    q_turned = in_hbm(jnp.swapaxes(q_start, 1, 2))
    o, h = lax.axis_index("outer"), lax.axis_index("hst")
    near = [(h & 1) * outer + (o ^ jnp.where(h & 1 == 1, turned(k), k)) for k in range(outer)]
    far = [(1 - (h & 1)) * outer + (o ^ jnp.where(h & 1 == 1, k, turned(k))) for k in range(outer)]

    def core(x):
        return exchange(x, lambda o, h, t: (o, h ^ 1, t))

    def chip(x, k):
        return exchange(x, lambda o, h, t: (o ^ (turned(k) if h % 2 else k), h, t))

    def after_all(value, places):
        value, *places = after(value, *places)
        return value, places

    left_far, left = mix(gradient, error_acc, q_turned, far[1:], near[1:], chunk)
    sent = (left + core(left_far).astype(F32)).astype(BF16)
    sent, (at_far, at_near) = after_all(sent, [far[0], near[0]])
    came = [chip(sent[(k - 1) * chunk:k * chunk], k) for k in range(1, outer)]
    left_far, left, mixed_own = mix(gradient, error_acc, q_turned, [at_far], [at_near], chunk, True)
    left = left + core(left_far).astype(F32)
    for part in came:
        left = left + part.astype(F32)
    for b in range(1, bits(hst)):
        bit = (h >> b) & 1
        sent = pick(left, 1 - bit).astype(BF16)
        left = pick(left, bit) + exchange(sent, lambda o, h, t, b=b: (o, h ^ (1 << b), t)).astype(F32)
    others = near[1:] + far[1:]
    early, late = len(others) // 3, len(others) // 2
    waiting, mixed = [others[:early], others[early:late]], []
    for b in range(bits(tp)):
        sent = left.astype(BF16)
        places = waiting.pop(0) if waiting else None
        if places:
            sent, places = after_all(sent, places)
            kept = keep(gradient, error_acc, places, chunk)
        got = exchange(sent, lambda o, h, t, b=b: (o, h, t ^ (1 << (b if h % 2 == 0 else bits(tp) - 1 - b))))
        if places:
            got, kept = after(got, kept)
            mixed.append(kept)
        left = sent.astype(F32) + got.astype(F32)
    mixed += [keep(gradient, error_acc, places, chunk) for places in waiting]
    own = left.astype(BF16)

    for b in reversed(range(1, bits(hst))):
        bit = (h >> b) & 1
        got = exchange(own, lambda o, h, t, b=b: (o, h ^ (1 << b), t))
        own = jnp.concatenate([jnp.where(bit == 1, got, own), jnp.where(bit == 1, own, got)])
    own, places = after_all(own, others[late:])
    near_left, far_left = [own], [core(own)]
    came = [chip(own, k) for k in range(1, outer)]
    right, gram_own = project([own, far_left[0]], [mixed_own], [(0, 1), (0, 0)])
    mixed.append(keep(gradient, error_acc, places, chunk))
    came[-1], right, mixed[2] = after(came[-1], right, mixed[2])
    near_left += came
    far_left += [core(part) for part in came]
    where = [(0, k) for k in range(early)] + [(1, k) for k in range(late - early)] + [(2, k) for k in range(len(others) - late)]
    n = outer - 1

    def project_others(lefts, chunks, right):
        used = sorted({store for store, _ in chunks})
        chunks = [(used.index(store), place) for store, place in chunks]
        return project(lefts, [mixed[store] for store in used], chunks, right)

    right, gram_near = project_others(near_left[1:], where[:n], right)
    right, gram_far = project_others(far_left[1:], where[n:], right)

    right, inverse = sum_right(right, (gram_own, gram_near, gram_far))
    left = jnp.zeros((rows, own.shape[1]), BF16)
    for place, part in zip(near + far, near_left + far_left):
        left = lax.dynamic_update_slice(left, part, (place * chunk, 0))
    return expand(left, inverse, right, 1.0 / (outer * hst))


def solution(mesh):
    in_specs = (
        P(("outer", "hst"), None, None, "tp"),
        P(("outer", "hst"), None, None, "tp"),
        P(None, "tp", None),
    )
    out_specs = P(None, None, "tp")
    return jax.shard_map(shards, mesh=mesh, in_specs=in_specs, out_specs=out_specs, check_vma=False)
```

```python
import jax
import jax.numpy as jnp
from jax import lax
from jax.experimental import pallas as pl
from jax.experimental.pallas import tpu as pltpu
from jax.sharding import PartitionSpec as P

AXES = ("outer", "hst", "tp")
PACK = 4
LANES = 128
F32, BF16 = jnp.float32, jnp.bfloat16
MIB = 1024 * 1024


def bits(size):
    return size.bit_length() - 1


def sizes():
    return tuple(lax.axis_size(axis) for axis in AXES)


def coordinates(index):
    _, hst, tp = sizes()
    return index // (hst * tp), index // tp % hst, index % tp


def exchange(x, partner):
    _, hst, tp = sizes()
    pairs = []
    for index in range(sizes()[0] * hst * tp):
        o, h, t = partner(*coordinates(index))
        pairs.append((index, (o * hst + h) * tp + t))
    return lax.ppermute(x, AXES, pairs)


def pick(x, index):
    half = x.shape[0] // 2
    return jnp.where(index == 1, x[half:], x[:half])


def params(mib):
    return pltpu.CompilerParams(vmem_limit_bytes=mib * MIB)


def cost():
    return pl.CostEstimate(flops=10**6, bytes_accessed=0, transcendentals=0)


def whole():
    return pl.BlockSpec(memory_space=pltpu.VMEM)


def in_hbm(x):
    return pltpu.with_memory_space_constraint(x, pltpu.HBM)


def scalar():
    return pl.BlockSpec(memory_space=pltpu.SMEM)


def load(starts, rows, g_hbm, e_hbm, g_ref, e_ref, sems):
    chunks = []
    for c, start in enumerate(starts):
        source = pl.ds(pl.multiple_of(start, rows), rows)
        where = pl.ds(c * rows, rows)
        copies = [
            pltpu.make_async_copy(hbm.at[:, :, source, :], ref.at[:, :, where, :], sems.at[k, c])
            for k, (hbm, ref) in enumerate(((g_hbm, g_ref), (e_hbm, e_ref)))
        ]
        chunks.append((where, copies))
    return chunks


def start_all(copies):
    for copy in copies:
        copy.start(priority=1)


def wait_all(copies):
    for copy in copies:
        copy.wait()


FETCHES = 4


def mix_kernel(place_ref, q_hbm, g_hbm, e_hbm, *refs):
    first_ref, second_ref = refs[:2]
    mixed_ref = refs[2] if len(refs) == 9 else None
    q_ref, g_ref, e_ref, wide_ref, q_sem, sems = refs[-6:]
    m_count, pack, total_rows, width = g_ref.shape
    rank = q_ref.shape[1]
    count = place_ref.shape[0]
    rows = total_rows // count
    q_copy = pltpu.make_async_copy(q_hbm, q_ref, q_sem)
    q_copy.start()
    chunks = load([place_ref[c] * rows for c in range(count)], rows, g_hbm, e_hbm, g_ref, e_ref, sems)
    for _, copies in chunks[:FETCHES]:
        start_all(copies)
    lane_group = lax.broadcasted_iota(jnp.int32, (width, LANES), 1) // rank
    q_copy.wait()
    for m in range(m_count):
        turned = jnp.concatenate([q_ref[m]] * pack, axis=0).T
        for j in range(pack):
            wide_ref[m, pl.ds(j * width, width), :] = jnp.where(lane_group == j, turned, 0.0).astype(BF16)
    for c, (where, copies) in enumerate(chunks):
        wait_all(copies)
        if c + FETCHES < count:
            start_all(chunks[c + FETCHES][1])
        left_ref = first_ref if c < count // 2 else second_ref
        at = pl.ds(c % (count // 2) * rows, rows)
        for m in range(m_count):
            mixed = [g_ref[m, j, where, :] + e_ref[m, j, where, :] for j in range(pack)]
            total = jnp.dot(jnp.concatenate(mixed, axis=1), wide_ref[m], preferred_element_type=F32)
            left_ref[at, m * LANES:(m + 1) * LANES] = total.astype(left_ref.dtype)
            if mixed_ref is not None:
                for j in range(pack):
                    mixed_ref[m, j, where, :] = mixed[j]


def mix(gradient, error_acc, q_turned, first, second, rows, kept=False):
    m_count, pack, _, width = gradient.shape
    places = jnp.stack(first + second).astype(jnp.int32)
    count = len(first + second)
    shape = (m_count, pack, count * rows, width)
    hbm = pl.BlockSpec(memory_space=pltpu.HBM)
    return pl.pallas_call(
        mix_kernel,
        in_specs=[scalar()] + [hbm] * 3,
        out_specs=[whole()] * (2 + kept),
        out_shape=[pltpu.VMEM((len(first) * rows, m_count * LANES), dtype) for dtype in (BF16, F32)] + [pltpu.VMEM(shape, BF16)] * kept,
        scratch_shapes=[
            pltpu.VMEM(q_turned.shape, F32),
            pltpu.VMEM(shape, BF16),
            pltpu.VMEM(shape, BF16),
            pltpu.VMEM((m_count, pack * width, LANES), BF16),
            pltpu.SemaphoreType.DMA,
            pltpu.SemaphoreType.DMA((2, count)),
        ],
        compiler_params=params(20),
        cost_estimate=cost(),
        name="mix",
    )(places, q_turned, gradient, error_acc)


def keep_kernel(place_ref, g_hbm, e_hbm, mixed_ref, g_ref, e_ref, sems):
    count = place_ref.shape[0]
    rows = g_ref.shape[2] // count
    chunks = load([place_ref[c] * rows for c in range(count)], rows, g_hbm, e_hbm, g_ref, e_ref, sems)
    for _, copies in chunks:
        start_all(copies)
    for where, copies in chunks:
        wait_all(copies)
        mixed_ref[:, :, where, :] = g_ref[:, :, where, :] + e_ref[:, :, where, :]


def keep(gradient, error_acc, places, rows):
    m_count, pack, _, width = gradient.shape
    count = len(places)
    shape = (m_count, pack, count * rows, width)
    return pl.pallas_call(
        keep_kernel,
        in_specs=[scalar()] + [pl.BlockSpec(memory_space=pltpu.HBM)] * 2,
        out_specs=whole(),
        out_shape=pltpu.VMEM(shape, BF16),
        scratch_shapes=[pltpu.VMEM(shape, BF16), pltpu.VMEM(shape, BF16), pltpu.SemaphoreType.DMA((2, count))],
        compiler_params=params(16),
        cost_estimate=cost(),
        name="keep",
    )(jnp.stack(places).astype(jnp.int32), gradient, error_acc)


def project_kernel(chunks, *refs):
    count = len(chunks)
    lefts, right_ref, gram_ref = refs[:count], refs[-2], refs[-1]
    stores = 1 + max(store for store, _ in chunks)
    mixed = refs[count:count + stores]
    before = refs[count + stores:-2]
    m_count, pack, _, width = mixed[0].shape
    rank = LANES // pack
    right = [before[0][m] if before else jnp.zeros((rank, width), F32) for m in range(m_count)]
    for c, (store, place) in enumerate(chunks):
        left = lefts[c][...]
        rows = left.shape[0]
        turned = left.T
        every = jnp.dot(turned, left, preferred_element_type=F32)
        for m in range(m_count):
            gram = jnp.zeros((rank, rank), F32)
            for j in range(pack):
                at = m * LANES + j * rank
                gram += every[at:at + rank, at:at + rank]
                block = mixed[store][m, j, pl.ds(place * rows, rows), :]
                right[m] += jnp.dot(turned[at:at + rank], block, preferred_element_type=F32)
            gram_ref[c, m] = gram
    for m in range(m_count):
        right_ref[m] = right[m]


def project(lefts, mixed, chunks, *before):
    m_count, pack, _, width = mixed[0].shape
    rank = LANES // pack
    mixed = [pltpu.with_memory_space_constraint(x, pltpu.VMEM) for x in mixed]
    return pl.pallas_call(
        lambda *refs: project_kernel(chunks, *refs),
        in_specs=[whole()] * (len(lefts) + len(mixed) + len(before)),
        out_specs=[whole()] * 2,
        out_shape=[pltpu.VMEM((m_count, rank, width), F32), pltpu.VMEM((len(lefts), m_count, rank, rank), F32)],
        compiler_params=params(8),
        cost_estimate=cost(),
        name="project",
    )(*lefts, *mixed, *before)


def tree_sum(parts):
    while len(parts) > 1:
        parts = [parts[k] + parts[k + 1] for k in range(0, len(parts), 2)]
    return parts[0]


def invert_kernel(steps, *refs):
    grams, held_ref = refs[:-1], refs[-1]
    m_count, rank, _ = held_ref.shape
    row_at = lax.broadcasted_iota(jnp.int32, (rank, rank), 0)
    col_at = lax.broadcasted_iota(jnp.int32, (rank, rank), 1)
    lane = lax.broadcasted_iota(jnp.int32, (1, rank), 1)
    held = [grams[0][m] for m in range(m_count)] if len(grams) == 1 else [
        tree_sum([grams[0][0, m]] + [grams[1][c, m] for c in range(grams[1].shape[0])])
        + tree_sum([grams[0][1, m]] + [grams[2][c, m] for c in range(grams[2].shape[0])])
        for m in range(m_count)
    ]
    for k in steps:
        for m in range(m_count):
            a = held[m]
            row, col = a[k:k + 1, :], a[:, k:k + 1]
            scaled = jnp.where(lane == k, 1.0, row) * (1.0 / a[k:k + 1, k:k + 1])
            held[m] = jnp.where(row_at == k, scaled, jnp.where(col_at == k, 0.0, a) - col * scaled)
    for m in range(m_count):
        held_ref[m] = held[m]


def invert(steps, *grams):
    return pl.pallas_call(
        lambda *refs: invert_kernel(steps, *refs),
        in_specs=[whole()] * len(grams),
        out_specs=whole(),
        out_shape=pltpu.VMEM(grams[0].shape[-3:], F32),
        compiler_params=params(4),
        cost_estimate=cost(),
        name="invert",
    )(*grams)


def three_parts(x):
    high = x.astype(BF16)
    rest = x - high.astype(F32)
    middle = rest.astype(BF16)
    return high, middle, (rest - middle.astype(F32)).astype(BF16)


def small_dot(a, b):
    a0, a1, a2 = three_parts(a)
    b0, b1, b2 = three_parts(b)
    wide = jnp.concatenate([a0, a0, a1, a1, a0, a2], axis=1)
    tall = jnp.concatenate([b0, b1, b0, b1, b2, b0], axis=0)
    return jnp.dot(wide, tall, preferred_element_type=F32)


EXPAND_ROWS = 512


def expand_kernel(scale, left_ref, inverse_ref, right_ref, update_ref, wide_ref, held_ref, sems):
    m_count, rank, width = right_ref.shape
    pack = LANES // rank
    copies = []
    for m in range(m_count):
        z = small_dot(inverse_ref[m], right_ref[m]) * scale
        high = z.astype(BF16)
        low = (z - high.astype(F32)).astype(BF16)
        wide_ref[m] = jnp.zeros(wide_ref.shape[1:], BF16)
        for j in range(pack):
            wide_ref[m, j, pl.ds(j * rank, rank), :] = high
            wide_ref[m, j, pl.ds(LANES + j * rank, rank), :] = low
            for p in range(left_ref.shape[0] // EXPAND_ROWS):
                where = pl.ds(p * EXPAND_ROWS, EXPAND_ROWS)
                left = left_ref[where, m * LANES:(m + 1) * LANES]
                rows = jnp.dot(jnp.concatenate([left, left], axis=1), wide_ref[m, j], preferred_element_type=F32)
                held_ref[m, j, where, :] = rows.astype(BF16)
                copy = pltpu.make_async_copy(held_ref.at[m, j, where, :], update_ref.at[m, j, where, :], sems.at[m, j, p])
                copy.start(priority=p % 2)
                copies.append(copy)
    wait_all(copies)


def expand(left, inverse, right, scale):
    m_count, rank, width = right.shape
    pack = LANES // rank
    rows = left.shape[0]
    shape = (m_count, pack, rows, width)
    out = pl.pallas_call(
        lambda *refs: expand_kernel(scale, *refs),
        in_specs=[whole()] * 3,
        out_specs=pl.BlockSpec(memory_space=pl.ANY),
        out_shape=jax.ShapeDtypeStruct(shape, BF16),
        scratch_shapes=[
            pltpu.VMEM((m_count, pack, 2 * LANES, width), BF16),
            pltpu.VMEM(shape, BF16),
            pltpu.SemaphoreType.DMA((m_count, pack, rows // EXPAND_ROWS)),
        ],
        compiler_params=params(20),
        name="expand",
    )(left, inverse, right)
    return out.reshape(m_count, pack * rows, width)


def sum_right(right, grams):
    outer, hst, _ = sizes()
    rank = right.shape[1]
    for b in range(bits(hst)):
        right = right + exchange(right, lambda o, h, t, b=b: (o, h ^ (1 << b), t))
    early = rank // 4
    right, inverse = after(right, invert(range(early), *grams))
    parts = [right] + [exchange(right, lambda o, h, t, k=k: (o ^ k, h, t)) for k in range(1, outer)]
    inverse = invert(range(early, rank), inverse)
    return tree_sum(parts), inverse


def after(value, *others):
    return lax.optimization_barrier((value, *others))


def shards(gradient, error_acc, q_start):
    _, m_count, depth, width = gradient.shape
    outer, hst, tp = sizes()
    rows = depth // PACK
    chunk = rows // (2 * outer)
    shape = (m_count, PACK, rows, width)
    gradient, error_acc = in_hbm(gradient.reshape(shape)), in_hbm(error_acc.reshape(shape))
    q_turned = in_hbm(jnp.swapaxes(q_start, 1, 2))
    o, h = lax.axis_index("outer"), lax.axis_index("hst")
    near = [(h & 1) * outer + (o ^ k) for k in range(outer)]
    far = [(1 - (h & 1)) * outer + (o ^ k) for k in range(outer)]

    def core(x):
        return exchange(x, lambda o, h, t: (o, h ^ 1, t))

    def chip(x, k):
        return exchange(x, lambda o, h, t: (o ^ k, h, t))

    def after_all(value, places):
        value, *places = after(value, *places)
        return value, places

    left_far, left = mix(gradient, error_acc, q_turned, far[1:], near[1:], chunk)
    sent = (left + core(left_far).astype(F32)).astype(BF16)
    sent, (at_far, at_near) = after_all(sent, [far[0], near[0]])
    came = [chip(sent[(k - 1) * chunk:k * chunk], k) for k in range(1, outer)]
    left_far, left, mixed_own = mix(gradient, error_acc, q_turned, [at_far], [at_near], chunk, True)
    left = left + core(left_far).astype(F32)
    for part in came:
        left = left + part.astype(F32)
    for b in range(1, bits(hst)):
        bit = (h >> b) & 1
        sent = pick(left, 1 - bit).astype(BF16)
        left = pick(left, bit) + exchange(sent, lambda o, h, t, b=b: (o, h ^ (1 << b), t)).astype(F32)
    others = near[1:] + far[1:]
    early, late = len(others) // 6, len(others) // 2
    waiting, mixed = [others[:early], others[early:late]], []
    for b in range(bits(tp)):
        sent = left.astype(BF16)
        places = waiting.pop(0) if waiting else None
        if places:
            sent, places = after_all(sent, places)
            kept = keep(gradient, error_acc, places, chunk)
        got = exchange(sent, lambda o, h, t, b=b: (o, h, t ^ (1 << (b if h % 2 == 0 else bits(tp) - 1 - b))))
        if places:
            got, kept = after(got, kept)
            mixed.append(kept)
        left = sent.astype(F32) + got.astype(F32)
    mixed += [keep(gradient, error_acc, places, chunk) for places in waiting]
    own = left.astype(BF16)

    for b in reversed(range(1, bits(hst))):
        bit = (h >> b) & 1
        got = exchange(own, lambda o, h, t, b=b: (o, h ^ (1 << b), t))
        own = jnp.concatenate([jnp.where(bit == 1, got, own), jnp.where(bit == 1, own, got)])
    own, places = after_all(own, others[late:])
    near_left, far_left = [own], [core(own)]
    came = [chip(own, k) for k in range(1, outer)]
    right, gram_own = project([own, far_left[0]], [mixed_own], [(0, 1), (0, 0)])
    mixed.append(keep(gradient, error_acc, places, chunk))
    came[-1], right, mixed[2] = after(came[-1], right, mixed[2])
    near_left += came
    far_left += [core(part) for part in came]
    where = [(0, k) for k in range(early)] + [(1, k) for k in range(late - early)] + [(2, k) for k in range(len(others) - late)]
    n = outer - 1

    def project_others(lefts, chunks, right):
        used = sorted({store for store, _ in chunks})
        chunks = [(used.index(store), place) for store, place in chunks]
        return project(lefts, [mixed[store] for store in used], chunks, right)

    right, gram_near = project_others(near_left[1:], where[:n], right)
    right, gram_far = project_others(far_left[1:], where[n:], right)

    right, inverse = sum_right(right, (gram_own, gram_near, gram_far))
    left = jnp.zeros((rows, own.shape[1]), BF16)
    for place, part in zip(near + far, near_left + far_left):
        left = lax.dynamic_update_slice(left, part, (place * chunk, 0))
    return expand(left, inverse, right, 1.0 / (outer * hst))


def solution(mesh):
    in_specs = (
        P(("outer", "hst"), None, None, "tp"),
        P(("outer", "hst"), None, None, "tp"),
        P(None, "tp", None),
    )
    out_specs = P(None, None, "tp")
    return jax.shard_map(shards, mesh=mesh, in_specs=in_specs, out_specs=out_specs, check_vma=False)
```
